32 devices in a mesh: band: 16 (over z, y, x), lon: 2 (over core).
Axes of the slice: x: 2, y: 2, z: 4, core: 2. Of those that a mesh axis runs over, the one named last changes fastest.
Arguments:
- background: float32 [2, 16, 256, 256], P(None, None, ('lon', 'band')), may hold values from -6 to 6
- scale_x: float32 [16, 256, 256], P(None, ('lon', 'band')), may hold values from 0.04 to 0.24
- scale_y: float32 [16, 256, 256], P(None, ('lon', 'band')), may hold values from 0.04 to 0.24
- filter_bands: float32 [2, 5, 16], replicated, may hold values from -0.3 to 0.3
- band_rows: int32 [16], replicated, may hold values from 8 to 32, as said below
Outputs:
- increment: float32 [2, 16, 256, 256], P(None, None, ('lon', 'band'))
- band_field: float32 [2, 16, 512, 256], P(None, None, 'band', 'lon')
The draws below stay inside these ranges and needn't reach their ends.
Inputs may be any that keep to these rules, and one draw needn't show every extreme that they name: `band_rows`: bands follow one another from the first row and their rows sum to 256; one band has exactly 32 rows and one exactly 8 rows.
All inputs are finite; a program needn't handle non-finite values.
Results may differ from the reference program's by a relative error of at most 0.0003.
Values sent between devices are 32-bit elements; how exact they have to be, the bound alone decides.
No kernel may reach another device: no remote copies, remote signals or barrier semaphores. Data moves between devices by JAX's collectives and lax.ppermute only.
A program may use at most 64 MiB of HBM per device.

```python
import math
import jax
import jax.numpy as jnp
from jax import lax

VARS = 2
LEVELS = 16
STEPS = 8
EDGE = 8
BAND_MEAN = 16
CAP = 32
NY = 256
NX = 256
N_BAND = 16


def draw_band_rows(key, part):
    first_key, second_key = jax.random.split(jax.random.fold_in(key, 7))
    others = N_BAND - 2
    spread_rows = BAND_MEAN // 8
    rough = jax.random.randint(first_key, (others,), 0, spread_rows + 1)
    rest = others * BAND_MEAN - EDGE
    base = rest // others
    remain = rest % others
    index = jnp.arange(others)
    change = rough - jnp.roll(rough, -1)
    middle = base + (index < remain).astype(jnp.int32) + change
    values = jnp.concatenate([jnp.array([CAP, EDGE], jnp.int32), middle.astype(jnp.int32)])
    places = jax.random.permutation(second_key, N_BAND)
    lengths = jnp.zeros((N_BAND,), jnp.int32).at[places].set(values)
    return lengths.astype(jnp.int32)


def level_of(stream_key, shape, cuts, smallest, largest):
    level, own = 1.0, jax.random.fold_in(stream_key, 6)
    for position, parts in cuts:
        steps = jnp.exp(jax.random.uniform(jax.random.fold_in(own, position), (parts,), jnp.float32, smallest / len(cuts), largest / len(cuts)))
        level = level * jnp.repeat(steps, shape[position] // parts).reshape([-1 if axis == position else 1 for axis in range(len(shape))])
    return level


def noise(key, shape, scale, reach, shards=(), held_as=jnp.bfloat16):
    entries = scale * jax.random.normal(key, shape, jnp.float32)
    if shards:
        entries = entries * level_of(key, shape, shards, -0.22, 0.18)
    return jnp.clip(entries, -reach, reach).astype(held_as)


def setup_inputs(seed: int = 0) -> dict:
    seeds = jax.random.split(jax.random.key(seed), 6)
    return {
        "background": noise(seeds[0], (VARS, LEVELS, NX, NY), 1.0, 6.0, ((2, 32),), jnp.float32),
        "scale_x": jnp.clip(jnp.exp(math.log(0.24) - 1.7917595 * jax.random.uniform(seeds[1], (LEVELS, NX, NY), jnp.float32) ** level_of(seeds[1], (LEVELS, NX, NY), ((1, 32),), -0.2, 0.2)), 0.04, 0.24),
        "scale_y": jnp.clip(jnp.exp(math.log(0.24) - 1.7917595 * jax.random.uniform(seeds[2], (LEVELS, NX, NY), jnp.float32) ** level_of(seeds[2], (LEVELS, NX, NY), ((1, 32),), -0.2, 0.2)), 0.04, 0.24),
        "filter_bands": jnp.clip(jax.random.uniform(seeds[3], (VARS, 5, LEVELS), jnp.float32, -0.3, 0.3), -0.3, 0.3),
        "band_rows": draw_band_rows(jax.random.fold_in(seeds[5], 71), 0),
    }


def spread(field, along_x, along_y, x_axis, y_axis):
    flux_x = along_x * (jnp.roll(field, -1, x_axis) - field)
    flux_y = along_y * (jnp.roll(field, -1, y_axis) - field)
    return field + flux_x - jnp.roll(flux_x, 1, x_axis) + flux_y - jnp.roll(flux_y, 1, y_axis)


def vertical(field, filter_bands):
    levels = field.shape[1]
    padded = jnp.pad(field, ((0, 0), (2, 2), (0, 0), (0, 0)))
    total = field
    for offset in range(5):
        weight = filter_bands[:, offset, :][:, :, None, None]
        total = total + weight * padded[:, offset:offset + levels]
    return total


def reference(background, scale_x, scale_y, filter_bands, band_rows):
    rows = background.shape[3]
    along_y = scale_y * (jnp.arange(rows) < rows - 1).astype(jnp.float32)
    field = background
    for step in range(STEPS):
        field = spread(field, scale_x, along_y, 2, 3)
    increment = vertical(field, filter_bands)
    starts = (jnp.cumsum(band_rows) - band_rows).astype(jnp.int32)
    padded = jnp.pad(increment, ((0, 0), (0, 0), (0, 0), (0, CAP)))

    def one_band(pair):
        piece = lax.dynamic_slice_in_dim(padded, pair[0], CAP, 3)
        keep = (jnp.arange(CAP) < pair[1]).astype(jnp.float32)
        return piece * keep

    bands = lax.map(one_band, (starts, band_rows.astype(jnp.int32)))
    band_field = jnp.transpose(bands, (1, 2, 0, 4, 3)).reshape(VARS, LEVELS, N_BAND * CAP, background.shape[2])
    return increment, band_field
```

```python
import functools
import math

import jax
import jax.numpy as jnp
from jax import lax
from jax.experimental import pallas as pl
from jax.experimental.pallas import tpu as pltpu
from jax.sharding import PartitionSpec as P

STEPS = 8
CAP = 32
LANES = 128
TAPS = 5
VMEM = pl.BlockSpec(memory_space=pltpu.VMEM)
SMEM = pl.BlockSpec(memory_space=pltpu.SMEM)
ANY = pl.BlockSpec(memory_space=pl.ANY)


def regroup_kernel(background, scale_x, scale_y, out, sems):
    variables, levels = background.shape[:2]
    groups = out.shape[0]
    part = levels // groups
    copies = []
    for q in range(groups):
        near = pl.ds(q * part, part)
        sources = [background.at[v, near] for v in range(variables)]
        sources += [scale_x.at[near], scale_y.at[near]]
        for i, source in enumerate(sources):
            copies.append(
                pltpu.make_async_copy(source, out.at[q, pl.ds(i * part, part)], sems.at[q, i])
            )
    for copy in copies:
        copy.start()
    for copy in copies:
        copy.wait()


def diffuse_kernel(
    groups, band_rows, low, mine, high, bands, *rest
):
    strips, field, along_x, along_y, result = rest[:groups], *rest[groups:]
    _, channels, width, rows = mine.shape
    part = channels // 4
    pairs = 2 * part
    sources = [low] + [mine.at[s] for s in range(groups)] + [high]
    columns = len(sources) * width
    inside = lax.broadcasted_iota(jnp.int32, (pairs, rows), 1) < rows - 1
    for s, source in enumerate(sources):
        flow = jnp.swapaxes(source[...], 0, 1)
        field[pl.ds(s * width, width)] = flow[:, :pairs]
        coef_x = flow[:, pairs : pairs + part]
        coef_y = flow[:, pairs + part :]
        along_x[pl.ds(s * width, width)] = jnp.concatenate([coef_x, coef_x], 1)
        coef_y = jnp.concatenate([coef_y, coef_y], 1)
        along_y[pl.ds(s * width, width)] = jnp.where(inside[None], coef_y, 0.0)

    for step in range(STEPS):
        first, last = step + 1, columns - 1 - step
        here = field[first]
        before = along_x[first - 1] * (here - field[first - 1])
        for c in range(first, last):
            after = field[c + 1]
            flux_x = along_x[c] * (after - here)
            flux_y = along_y[c] * (pltpu.roll(here, rows - 1, 1) - here)
            field[c] = here + flux_x - before + flux_y - pltpu.roll(flux_y, 1, 1)
            here, before = after, flux_x

    me = lax.rem(lax.axis_index("band"), groups)
    for s in range(groups):
        block = jnp.swapaxes(field[pl.ds((s + 1) * width, width)], 0, 1)
        for half in range(rows // LANES):
            result[half, :, pl.ds(s * width, width)] = block[:, :, half * LANES : (half + 1) * LANES]
        strips_block = block
        for k in range(groups):
            @pl.when(jnp.bitwise_xor(me, k) == s)
            def _(k=k, strips_block=strips_block):
                strips[k][...] = strips_block

    halves = rows // LANES
    lane = lax.broadcasted_iota(jnp.int32, (groups * width, LANES), 1)

    def one_band(b, start):
        half = start // LANES
        offset = start - half * LANES
        beyond = lax.rem(half + 1, halves)
        for v in range(2):
            packed = None
            for l in range(part):
                i = v * part + l
                window = jnp.where(lane >= offset, result[half, i], result[beyond, i])
                shift = lax.rem(LANES + l * CAP - offset, LANES)
                turned = pltpu.roll(window, shift, 1)
                packed = turned if l == 0 else jnp.where(lane >= l * CAP, turned, packed)
            bands[b, v] = packed
        return start + band_rows[b]

    lax.fori_loop(0, bands.shape[0], one_band, jnp.int32(0))


def filtered(weights, v, l, levels, at):
    total = at(v, l)
    for tap in range(TAPS):
        other = l + tap - TAPS // 2
        if 0 <= other < levels:
            total = total + weights[v, tap, l] * at(v, other)
    return total


def increment_kernel(groups, weights, *refs):
    pieces, out, whole = refs[:groups], refs[groups], refs[groups + 1]
    variables, levels = out.shape[:2]
    part = levels // groups
    me = lax.rem(lax.axis_index("band"), groups)
    for k in range(groups):
        near = pl.ds(jnp.bitwise_xor(me, k) * part, part)
        for v in range(variables):
            whole[v, near] = pieces[k][pl.ds(v * part, part)]
    for v in range(variables):
        for l in range(levels):
            out[v, l] = filtered(weights, v, l, levels, lambda a, b: whole[a, b])


def band_kernel(groups, band_rows, weights, arrived, out, whole):
    variables, levels, height, columns = out.shape
    part = levels // groups
    count = arrived.shape[0]
    here = band_rows[lax.axis_index("band")]
    for v in range(variables):
        for q in range(groups):
            tall = jnp.concatenate([arrived[s, v] for s in range(q, count, groups)], 0)
            flat = jnp.transpose(tall)
            for l in range(part):
                whole[v, q * part + l] = flat[l * height : (l + 1) * height]
    keep = lax.broadcasted_iota(jnp.int32, (height, columns), 0) < here
    for v in range(variables):
        for l in range(levels):
            total = filtered(weights, v, l, levels, lambda a, b: whole[a, b])
            out[v, l] = jnp.where(keep, total, 0.0)


def shards(mesh_shape, background, scale_x, scale_y, filter_bands, band_rows):
    variables, levels, width, rows = background.shape
    count, blocks = mesh_shape["band"], mesh_shape["lon"]
    groups = math.isqrt(count)
    part = levels // groups
    channels = (variables + 2) * part
    f32 = jnp.float32

    def struct(*shape):
        return jax.ShapeDtypeStruct(shape, f32)

    parted = pl.pallas_call(
        regroup_kernel,
        out_shape=struct(groups, channels, width, rows),
        in_specs=[ANY] * 3,
        out_specs=ANY,
        scratch_shapes=[pltpu.SemaphoreType.DMA((groups, variables + 2))],
        name="regroup",
    )(background, scale_x, scale_y)
    near = [[g * groups + i for i in range(groups)] for g in range(count // groups)]
    mine = lax.all_to_all(
        parted, "band", split_axis=0, concat_axis=0, tiled=True, axis_index_groups=near
    )

    def shifted(by):
        total = count * blocks
        pairs = []
        for source in range(total):
            target = (source + by) % total
            pairs.append(
                (
                    source % count * blocks + source // count,
                    target % count * blocks + target // count,
                )
            )
        return pairs

    axes = ("band", "lon")
    low = lax.ppermute(mine[groups - 1], axes, shifted(groups))
    high = lax.ppermute(mine[0], axes, shifted(-groups))
    span = groups * width
    wide = (groups + 2) * width
    outs = pl.pallas_call(
        functools.partial(diffuse_kernel, groups),
        out_shape=[struct(count, variables, span, LANES)]
        + [struct(variables * part, width, rows)] * groups,
        in_specs=[SMEM] + [VMEM] * 3,
        out_specs=[VMEM] * (groups + 1),
        scratch_shapes=[pltpu.VMEM((wide, variables * part, rows), f32)] * 3
        + [pltpu.VMEM((rows // LANES, variables * part, span, LANES), f32)],
        name="diffuse",
    )(band_rows, low, mine, high)
    bands, strips = outs[0], outs[1:]
    arrived = lax.all_to_all(bands, "band", split_axis=0, concat_axis=0, tiled=True)
    pieces = [strips[0]] + [
        lax.ppermute(strips[k], "band", [(i, i ^ k) for i in range(count)])
        for k in range(1, groups)
    ]
    increment = pl.pallas_call(
        functools.partial(increment_kernel, groups),
        out_shape=struct(*background.shape),
        in_specs=[SMEM] + [VMEM] * groups,
        out_specs=VMEM,
        scratch_shapes=[pltpu.VMEM((variables, levels, width, rows), f32)],
        name="increment",
    )(filter_bands, *pieces)
    band_field = pl.pallas_call(
        functools.partial(band_kernel, groups),
        out_shape=struct(variables, levels, CAP, count * width),
        in_specs=[SMEM, SMEM, VMEM],
        out_specs=VMEM,
        scratch_shapes=[pltpu.VMEM((variables, levels, CAP, count * width), f32)],
        name="bands",
    )(band_rows, filter_bands, arrived)
    return increment, band_field


def solution(mesh):
    in_specs = (
        P(None, None, ("lon", "band"), None),
        P(None, ("lon", "band"), None),
        P(None, ("lon", "band"), None),
        P(),
        P(),
    )
    out_specs = (P(None, None, ("lon", "band"), None), P(None, None, "band", "lon"))
    return jax.shard_map(
        functools.partial(shards, dict(mesh.shape)),
        mesh=mesh,
        in_specs=in_specs,
        out_specs=out_specs,
        check_vma=False,
    )
```

```python
import functools
import math

import jax
import jax.numpy as jnp
from jax import lax
from jax.experimental import pallas as pl
from jax.experimental.pallas import tpu as pltpu
from jax.sharding import PartitionSpec as P

STEPS = 8
CAP = 32
LANES = 128
TAPS = 5
BLOCK = 16
UNROLL = 4
VMEM = pl.BlockSpec(memory_space=pltpu.VMEM)
SMEM = pl.BlockSpec(memory_space=pltpu.SMEM)


def regroup_kernel(background, scale_x, scale_y, out):
    variables, levels = background.shape[:2]
    groups = out.shape[0]
    part = levels // groups
    for q in range(groups):
        near = pl.ds(q * part, part)
        sources = [background[v, near] for v in range(variables)]
        sources += [scale_x[near], scale_y[near]]
        out[q] = jnp.swapaxes(jnp.concatenate(sources, 0), 0, 1)


def diffuse_kernel(groups, band_rows, low, mine, high, bands, *rest):
    strips, field, along_x, along_y, down_y, result = rest[:groups], *rest[groups:]
    _, width, channels, rows = mine.shape
    part = channels // 4
    pairs = 2 * part
    sources = [low] + [mine.at[s] for s in range(groups)] + [high]
    columns = len(sources) * width
    upper = lax.broadcasted_iota(jnp.int32, (1, pairs, rows), 1) < part
    inside = lax.broadcasted_iota(jnp.int32, (1, pairs, rows), 2) < rows - 1
    for s, source in enumerate(sources):
        near = pl.ds(s * width, width)
        field[near] = source[:, :pairs]
        coefs = source[:, pairs:]
        swapped = pltpu.roll(coefs, part, 1)
        along_x[near] = jnp.where(upper, coefs, swapped)
        flow_y = jnp.where(inside, jnp.where(upper, swapped, coefs), 0.0)
        along_y[near] = flow_y
        down_y[near] = pltpu.roll(flow_y, 1, 2)

    for step in range(STEPS):
        first, last = step + 1, columns - 1 - step
        before = along_x[first - 1] * (field[first] - field[first - 1])
        for c in range(first, last, BLOCK):
            m = min(BLOCK, last - c)
            near = pl.ds(c, m)
            both = field[pl.ds(c, m + 1)]
            here, after = both[:m], both[1:]
            flux_x = along_x[near] * (after - here)
            left = jnp.concatenate([before[None], flux_x[:-1]], 0)
            flux_y = along_y[near] * (pltpu.roll(here, rows - 1, 2) - here)
            under = down_y[near] * (here - pltpu.roll(here, 1, 2))
            field[near] = here + flux_x - left + flux_y - under
            before = flux_x[m - 1]

    me = lax.rem(lax.axis_index("band"), groups)
    halves = rows // LANES
    for s in range(groups):
        block = jnp.swapaxes(field[pl.ds((s + 1) * width, width)], 0, 1)
        for half in range(halves):
            result[half, :, pl.ds(s * width, width)] = block[:, :, half * LANES : (half + 1) * LANES]
    for k in range(groups):
        s = jnp.bitwise_xor(me, k)
        for half in range(halves):
            strips[k][:, :, half * LANES : (half + 1) * LANES] = result[
                half, :, pl.ds(pl.multiple_of(s * width, width), width)
            ]

    lane = lax.broadcasted_iota(jnp.int32, (groups * width, LANES), 1)

    def one_band(b, start):
        half = start // LANES
        offset = start - half * LANES
        beyond = lax.rem(half + 1, halves)
        for v in range(2):
            packed = None
            for l in range(part):
                i = v * part + l
                window = jnp.where(lane >= offset, result[half, i], result[beyond, i])
                shift = lax.rem(LANES + l * CAP - offset, LANES)
                turned = pltpu.roll(window, shift, 1)
                packed = turned if l == 0 else jnp.where(lane >= l * CAP, turned, packed)
            bands[b, v] = packed
        return start + band_rows[b]

    lax.fori_loop(0, bands.shape[0], one_band, jnp.int32(0), unroll=UNROLL)


def filtered(weights, v, l, levels, at):
    total = at(v, l)
    for tap in range(TAPS):
        other = l + tap - TAPS // 2
        if 0 <= other < levels:
            total = total + weights[v, tap, l] * at(v, other)
    return total


def increment_kernel(groups, weights, *refs):
    pieces, out, whole = refs[:groups], refs[groups], refs[groups + 1]
    variables, levels = out.shape[:2]
    part = levels // groups
    me = lax.rem(lax.axis_index("band"), groups)
    for k in range(groups):
        near = pl.ds(jnp.bitwise_xor(me, k) * part, part)
        for v in range(variables):
            whole[v, near] = pieces[k][pl.ds(v * part, part)]
    for v in range(variables):
        for l in range(levels):
            out[v, l] = filtered(weights, v, l, levels, lambda a, b: whole[a, b])


def band_kernel(groups, band_rows, weights, arrived, out, whole):
    variables, levels, height, columns = out.shape
    part = levels // groups
    count = arrived.shape[0]
    here = band_rows[lax.axis_index("band")]
    for v in range(variables):
        for q in range(groups):
            tall = jnp.concatenate([arrived[s, v] for s in range(q, count, groups)], 0)
            flat = jnp.transpose(tall)
            for l in range(part):
                whole[v, q * part + l] = flat[l * height : (l + 1) * height]
    keep = lax.broadcasted_iota(jnp.int32, (height, columns), 0) < here
    for v in range(variables):
        for l in range(levels):
            total = filtered(weights, v, l, levels, lambda a, b: whole[a, b])
            out[v, l] = jnp.where(keep, total, 0.0)


def shards(mesh_shape, background, scale_x, scale_y, filter_bands, band_rows):
    variables, levels, width, rows = background.shape
    count, blocks = mesh_shape["band"], mesh_shape["lon"]
    groups = math.isqrt(count)
    part = levels // groups
    channels = (variables + 2) * part
    f32 = jnp.float32

    def struct(*shape):
        return jax.ShapeDtypeStruct(shape, f32)

    parted = pl.pallas_call(
        regroup_kernel,
        out_shape=struct(groups, width, channels, rows),
        in_specs=[VMEM] * 3,
        out_specs=VMEM,
        name="regroup",
    )(background, scale_x, scale_y)
    near = [[g * groups + i for i in range(groups)] for g in range(count // groups)]
    mine = lax.all_to_all(
        parted, "band", split_axis=0, concat_axis=0, tiled=True, axis_index_groups=near
    )

    def shifted(by):
        total = count * blocks
        pairs = []
        for source in range(total):
            target = (source + by) % total
            pairs.append(
                (
                    source % count * blocks + source // count,
                    target % count * blocks + target // count,
                )
            )
        return pairs

    axes = ("band", "lon")
    low = lax.ppermute(mine[groups - 1], axes, shifted(groups))
    high = lax.ppermute(mine[0], axes, shifted(-groups))
    span = groups * width
    wide = (groups + 2) * width
    outs = pl.pallas_call(
        functools.partial(diffuse_kernel, groups),
        out_shape=[struct(count, variables, span, LANES)]
        + [struct(variables * part, width, rows)] * groups,
        in_specs=[SMEM] + [VMEM] * 3,
        out_specs=[VMEM] * (groups + 1),
        scratch_shapes=[pltpu.VMEM((wide, variables * part, rows), f32)] * 4
        + [pltpu.VMEM((rows // LANES, variables * part, span, LANES), f32)],
        name="diffuse",
    )(band_rows, low, mine, high)
    bands, strips = outs[0], outs[1:]
    arrived = lax.all_to_all(bands, "band", split_axis=0, concat_axis=0, tiled=True)
    pieces = [strips[0]] + [
        lax.ppermute(strips[k], "band", [(i, i ^ k) for i in range(count)])
        for k in range(1, groups)
    ]
    increment = pl.pallas_call(
        functools.partial(increment_kernel, groups),
        out_shape=struct(*background.shape),
        in_specs=[SMEM] + [VMEM] * groups,
        out_specs=VMEM,
        scratch_shapes=[pltpu.VMEM((variables, levels, width, rows), f32)],
        name="increment",
    )(filter_bands, *pieces)
    band_field = pl.pallas_call(
        functools.partial(band_kernel, groups),
        out_shape=struct(variables, levels, CAP, count * width),
        in_specs=[SMEM, SMEM, VMEM],
        out_specs=VMEM,
        scratch_shapes=[pltpu.VMEM((variables, levels, CAP, count * width), f32)],
        name="bands",
    )(band_rows, filter_bands, arrived)
    return increment, band_field


def solution(mesh):
    in_specs = (
        P(None, None, ("lon", "band"), None),
        P(None, ("lon", "band"), None),
        P(None, ("lon", "band"), None),
        P(),
        P(),
    )
    out_specs = (P(None, None, ("lon", "band"), None), P(None, None, "band", "lon"))
    return jax.shard_map(
        functools.partial(shards, dict(mesh.shape)),
        mesh=mesh,
        in_specs=in_specs,
        out_specs=out_specs,
        check_vma=False,
    )
```

```python
import functools
import math

import jax
import jax.numpy as jnp
from jax import lax
from jax.experimental import pallas as pl
from jax.experimental.pallas import tpu as pltpu
from jax.sharding import PartitionSpec as P

STEPS = 8
CAP = 32
LANES = 128
TAPS = 5
BLOCK = 16
UNROLL = 4
VMEM = pl.BlockSpec(memory_space=pltpu.VMEM)
SMEM = pl.BlockSpec(memory_space=pltpu.SMEM)
HBM = pl.BlockSpec(memory_space=pltpu.HBM)
ROOM = pltpu.CompilerParams(vmem_limit_bytes=8 * 2**20)


def regroup_kernel(background, scale_x, scale_y, out, field, along_x, along_y, sems):
    variables, levels = background.shape[:2]
    groups = out.shape[0]
    part = levels // groups
    copies = []
    for q in range(groups):
        near = pl.ds(q * part, part)
        copies.append(
            [
                pltpu.make_async_copy(background.at[:, near], field.at[:, near], sems.at[q, 0]),
                pltpu.make_async_copy(scale_x.at[near], along_x.at[near], sems.at[q, 1]),
                pltpu.make_async_copy(scale_y.at[near], along_y.at[near], sems.at[q, 2]),
            ]
        )
        for copy in copies[q]:
            copy.start()
    for q in range(groups):
        near = pl.ds(q * part, part)
        for copy in copies[q]:
            copy.wait()
        sources = [field[v, near] for v in range(variables)]
        sources += [along_x[near], along_y[near]]
        out[q] = jnp.swapaxes(jnp.concatenate(sources, 0), 0, 1)


def spread_out(source, near, field, along_x, along_y, down_y):
    _, channels, rows = source.shape
    part = channels // 4
    pairs = 2 * part
    upper = lax.broadcasted_iota(jnp.int32, (1, pairs, rows), 1) < part
    inside = lax.broadcasted_iota(jnp.int32, (1, pairs, rows), 2) < rows - 1
    field[near] = source[:, :pairs]
    coefs = source[:, pairs:]
    swapped = pltpu.roll(coefs, part, 1)
    along_x[near] = jnp.where(upper, coefs, swapped)
    flow_y = jnp.where(inside, jnp.where(upper, swapped, coefs), 0.0)
    along_y[near] = flow_y
    down_y[near] = pltpu.roll(flow_y, 1, 2)


def advance(field, along_x, along_y, down_y, first, last, before, behind):
    rows = field.shape[-1]
    if before is None:
        before = along_x[first - 1] * (field[first] - field[first - 1])
    entry = before
    for c in range(first, last, BLOCK):
        m = min(BLOCK, last - c)
        near = pl.ds(c, m)
        if c + m == last and behind is not None:
            here = field[near]
            after = here[1:]
            ahead = [along_x[pl.ds(c, m - 1)] * (after - here[:-1]), behind[None]]
            flux_x = jnp.concatenate(ahead, 0)
        else:
            both = field[pl.ds(c, m + 1)]
            here, after = both[:m], both[1:]
            flux_x = along_x[near] * (after - here)
        left = jnp.concatenate([before[None], flux_x[:-1]], 0)
        flux_y = along_y[near] * (pltpu.roll(here, rows - 1, 2) - here)
        under = down_y[near] * (here - pltpu.roll(here, 1, 2))
        field[near] = here + flux_x - left + flux_y - under
        before = flux_x[m - 1]
    return entry, before


def turn(columns, result, at):
    block = jnp.swapaxes(columns, 0, 1)
    for half in range(result.shape[0]):
        result[half, :, at] = block[:, :, half * LANES : (half + 1) * LANES]


def pack(result, band_rows, bands, at):
    halves, channels, count, _ = result.shape
    part = channels // 2
    lane = lax.broadcasted_iota(jnp.int32, (count, LANES), 1)

    def one_band(b, start):
        half = start // LANES
        offset = start - half * LANES
        beyond = lax.rem(half + 1, halves)
        for v in range(2):
            packed = None
            for l in range(part):
                i = v * part + l
                window = jnp.where(lane >= offset, result[half, i], result[beyond, i])
                shift = lax.rem(LANES + l * CAP - offset, LANES)
                turned = pltpu.roll(window, shift, 1)
                packed = turned if l == 0 else jnp.where(lane >= l * CAP, turned, packed)
            for source, target in at:
                bands[b, v, target] = packed[source]
        return start + band_rows[b]

    lax.fori_loop(0, bands.shape[0], one_band, jnp.int32(0), unroll=UNROLL)


def inner_kernel(band_rows, mine, field, along_x, along_y, down_y, sides, result, bands):
    groups, width, channels, rows = mine.shape
    for s in range(groups):
        spread_out(mine.at[s], pl.ds(s * width, width), field, along_x, along_y, down_y)
    span = groups * width
    for step in range(STEPS):
        entry, leave = advance(
            field, along_x, along_y, down_y, step + 1, span - 1 - step, None, None
        )
        sides[0, step] = entry
        sides[1, step] = leave
    for s in range(1, groups - 1):
        turn(field[pl.ds(s * width, width)], result, pl.ds((s - 1) * width, width))
    pack(result, band_rows, bands, [(slice(None), slice(None))])


def outer_kernel(groups, band_rows, low, high, *refs):
    inner, sides, inner_result, inner_bands, bands = refs[:4], *refs[4:8]
    strips = refs[8 : 8 + groups]
    ends, result, whole = refs[8 + groups : 12 + groups], *refs[12 + groups :]
    width, _, rows = low.shape
    span = groups * width
    for side, (halo, own) in enumerate(((low, 0), (high, span - width))):
        arrays = [end.at[side] for end in ends]
        spread_out(halo, pl.ds(side * width, width), *arrays)
        for end, array in zip(arrays, inner):
            end[pl.ds((1 - side) * width, width)] = array[pl.ds(own, width)]
    for step in range(STEPS):
        first = step + 1
        arrays = [end.at[0] for end in ends]
        advance(*arrays, first, first + width, None, sides[0, step])
        first = width - 1 - step
        arrays = [end.at[1] for end in ends]
        advance(*arrays, first, first + width, sides[1, step], None)
    field = ends[0]
    turn(field[0, pl.ds(width, width)], result, pl.ds(0, width))
    turn(field[1, pl.ds(0, width)], result, pl.ds(width, width))

    me = lax.rem(lax.axis_index("band"), groups)
    whole[:, :, pl.ds(width, span - 2 * width)] = inner_result[...]
    whole[:, :, pl.ds(0, width)] = result[:, :, pl.ds(0, width)]
    whole[:, :, pl.ds(span - width, width)] = result[:, :, pl.ds(width, width)]
    for k in range(groups):
        s = jnp.bitwise_xor(me, k)
        for half in range(rows // LANES):
            strips[k][:, :, half * LANES : (half + 1) * LANES] = whole[
                half, :, pl.ds(pl.multiple_of(s * width, width), width)
            ]

    bands[:, :, pl.ds(width, span - 2 * width)] = inner_bands[...]
    edges = [
        (slice(0, width), pl.ds(0, width)),
        (slice(width, 2 * width), pl.ds(span - width, width)),
    ]
    pack(result, band_rows, bands, edges)


def filtered(weights, v, l, levels, at):
    total = at(v, l)
    for tap in range(TAPS):
        other = l + tap - TAPS // 2
        if 0 <= other < levels:
            total = total + weights[tap, v, l] * at(v, other)
    return total


def increment_kernel(groups, weights, *refs):
    pieces, out, whole = refs[:groups], refs[groups], refs[groups + 1]
    variables, levels = out.shape[:2]
    part = levels // groups
    me = lax.rem(lax.axis_index("band"), groups)
    for k in range(groups):
        near = pl.ds(jnp.bitwise_xor(me, k) * part, part)
        for v in range(variables):
            whole[v, near] = pieces[k][pl.ds(v * part, part)]
    for v in range(variables):
        for l in range(levels):
            out[v, l] = filtered(weights, v, l, levels, lambda a, b: whole[a, b])


def band_kernel(groups, band_rows, weights, arrived, out, whole, ready, sems):
    variables, levels, height, columns = out.shape
    part = levels // groups
    count = arrived.shape[0]
    here = band_rows[lax.axis_index("band")]
    keep = lax.broadcasted_iota(jnp.int32, (height, columns), 0) < here
    copies = []
    for v in range(variables):
        for q in range(groups):
            tall = jnp.concatenate([arrived[s, v] for s in range(q, count, groups)], 0)
            flat = jnp.transpose(tall)
            for l in range(part):
                whole[v, q * part + l] = flat[l * height : (l + 1) * height]
        for l in range(levels):
            total = filtered(weights, v, l, levels, lambda a, b: whole[a, b])
            ready[v, l] = jnp.where(keep, total, 0.0)
        copies.append(pltpu.make_async_copy(ready.at[v], out.at[v], sems.at[v]))
        copies[v].start()
    for copy in copies:
        copy.wait()


def shards(mesh_shape, background, scale_x, scale_y, filter_bands, band_rows):
    variables, levels, width, rows = background.shape
    count, blocks = mesh_shape["band"], mesh_shape["lon"]
    groups = math.isqrt(count)
    part = levels // groups
    channels = (variables + 2) * part
    f32 = jnp.float32

    def struct(*shape):
        return jax.ShapeDtypeStruct(shape, f32)

    parted = pl.pallas_call(
        regroup_kernel,
        out_shape=struct(groups, width, channels, rows),
        in_specs=[HBM] * 3,
        out_specs=VMEM,
        scratch_shapes=[pltpu.VMEM(a.shape, f32) for a in (background, scale_x, scale_y)]
        + [pltpu.SemaphoreType.DMA((groups, 3))],
        compiler_params=ROOM,
        name="regroup",
    )(*(pltpu.with_memory_space_constraint(a, pltpu.HBM) for a in (background, scale_x, scale_y)))
    weights = jnp.transpose(filter_bands, (1, 0, 2))
    near = [[g * groups + i for i in range(groups)] for g in range(count // groups)]
    mine = lax.all_to_all(
        parted, "band", split_axis=0, concat_axis=0, tiled=True, axis_index_groups=near
    )

    def shifted(by):
        total = count * blocks
        pairs = []
        for source in range(total):
            target = (source + by) % total
            pairs.append(
                (
                    source % count * blocks + source // count,
                    target % count * blocks + target // count,
                )
            )
        return pairs

    axes = ("band", "lon")
    low = lax.ppermute(mine[groups - 1], axes, shifted(groups))
    high = lax.ppermute(mine[0], axes, shifted(-groups))
    span = groups * width
    inside = span - 2 * width
    halves = rows // LANES
    both = variables * part
    inner = pl.pallas_call(
        inner_kernel,
        out_shape=[struct(span, both, rows)] * 4
        + [
            struct(2, STEPS, both, rows),
            struct(halves, both, inside, LANES),
            struct(count, variables, inside, LANES),
        ],
        in_specs=[SMEM, VMEM],
        out_specs=[VMEM] * 7,
        compiler_params=ROOM,
        cost_estimate=pl.CostEstimate(
            flops=20 * STEPS * span * both * rows, bytes_accessed=2**20, transcendentals=0
        ),
        name="inner",
    )(band_rows, mine)
    outs = pl.pallas_call(
        functools.partial(outer_kernel, groups),
        out_shape=[struct(count, variables, span, LANES)] + [struct(both, width, rows)] * groups,
        in_specs=[SMEM] + [VMEM] * 9,
        out_specs=[VMEM] * (groups + 1),
        scratch_shapes=[pltpu.VMEM((2, 2 * width, both, rows), f32)] * 4
        + [
            pltpu.VMEM((halves, both, 2 * width, LANES), f32),
            pltpu.VMEM((halves, both, span, LANES), f32),
        ],
        compiler_params=ROOM,
        name="outer",
    )(band_rows, low, high, *inner)
    bands, strips = outs[0], outs[1:]
    arrived = lax.all_to_all(bands, "band", split_axis=0, concat_axis=0, tiled=True)
    pieces = [strips[0]] + [
        lax.ppermute(strips[k], "band", [(i, i ^ k) for i in range(count)])
        for k in range(1, groups)
    ]
    increment = pl.pallas_call(
        functools.partial(increment_kernel, groups),
        out_shape=struct(*background.shape),
        in_specs=[SMEM] + [VMEM] * groups,
        out_specs=VMEM,
        scratch_shapes=[pltpu.VMEM((variables, levels, width, rows), f32)],
        compiler_params=ROOM,
        name="increment",
    )(weights, *pieces)
    band_field = pl.pallas_call(
        functools.partial(band_kernel, groups),
        out_shape=struct(variables, levels, CAP, count * width),
        in_specs=[SMEM, SMEM, VMEM],
        out_specs=HBM,
        scratch_shapes=[pltpu.VMEM((variables, levels, CAP, count * width), f32)] * 2
        + [pltpu.SemaphoreType.DMA((variables,))],
        compiler_params=ROOM,
        name="bands",
    )(band_rows, weights, arrived)
    return increment, band_field


def solution(mesh):
    in_specs = (
        P(None, None, ("lon", "band"), None),
        P(None, ("lon", "band"), None),
        P(None, ("lon", "band"), None),
        P(),
        P(),
    )
    out_specs = (P(None, None, ("lon", "band"), None), P(None, None, "band", "lon"))
    return jax.shard_map(
        functools.partial(shards, dict(mesh.shape)),
        mesh=mesh,
        in_specs=in_specs,
        out_specs=out_specs,
        check_vma=False,
    )
```

```python
import functools
import math

import jax
import jax.numpy as jnp
from jax import lax
from jax.experimental import pallas as pl
from jax.experimental.pallas import tpu as pltpu
from jax.sharding import PartitionSpec as P

STEPS = 8
CAP = 32
LANES = 128
TAPS = 5
BLOCK = 16
VMEM = pl.BlockSpec(memory_space=pltpu.VMEM)
SMEM = pl.BlockSpec(memory_space=pltpu.SMEM)
HBM = pl.BlockSpec(memory_space=pltpu.HBM)
ROOM = pltpu.CompilerParams(vmem_limit_bytes=8 * 2**20)


def regroup_kernel(background, scale_x, scale_y, out, field, along_x, along_y, sems):
    variables, levels = background.shape[:2]
    groups = out.shape[0]
    part = levels // groups
    copies = []
    for q in range(groups):
        near = pl.ds(q * part, part)
        copies.append(
            [
                pltpu.make_async_copy(background.at[:, near], field.at[:, near], sems.at[q, 0]),
                pltpu.make_async_copy(scale_x.at[near], along_x.at[near], sems.at[q, 1]),
                pltpu.make_async_copy(scale_y.at[near], along_y.at[near], sems.at[q, 2]),
            ]
        )
        for copy in copies[q]:
            copy.start()
    for q in range(groups):
        near = pl.ds(q * part, part)
        for copy in copies[q]:
            copy.wait()
        sources = [field[v, near] for v in range(variables)]
        sources += [along_x[near], along_y[near]]
        out[q] = jnp.swapaxes(jnp.concatenate(sources, 0), 0, 1)


def spread_out(source, near, field, along_x, along_y, down_y):
    _, channels, rows = source.shape
    part = channels // 4
    pairs = 2 * part
    upper = lax.broadcasted_iota(jnp.int32, (1, pairs, rows), 1) < part
    inside = lax.broadcasted_iota(jnp.int32, (1, pairs, rows), 2) < rows - 1
    field[near] = source[:, :pairs]
    coefs = source[:, pairs:]
    swapped = pltpu.roll(coefs, part, 1)
    along_x[near] = jnp.where(upper, coefs, swapped)
    flow_y = jnp.where(inside, jnp.where(upper, swapped, coefs), 0.0)
    along_y[near] = flow_y
    down_y[near] = pltpu.roll(flow_y, 1, 2)


def advance(parts):
    joined, fluxes, ends = [], [], []
    for field, along_x, along_y, down_y, first, last, before, behind in parts:
        near = pl.ds(first, last - first)
        here = field[near]
        inner = along_x[pl.ds(first, last - first - 1)] * (here[1:] - here[:-1])
        if before is None:
            before = along_x[first - 1] * (here[0] - field[first - 1])
        if behind is None:
            behind = along_x[last - 1] * (field[last] - here[-1])
        fluxes.append((before, behind))
        entering = jnp.concatenate([before[None], inner], 0)
        leaving = jnp.concatenate([inner, behind[None]], 0)
        joined.append((here, leaving, entering, along_y[near], down_y[near]))
        ends.append(sum(ends[-1:]) + last - first)
    here, leaving, entering, up, down = (jnp.concatenate(each, 0) for each in zip(*joined))
    rows = here.shape[-1]
    flux_y = up * (pltpu.roll(here, rows - 1, 2) - here)
    under = down * (here - pltpu.roll(here, 1, 2))
    result = here + leaving - entering + flux_y - under
    for (field, _, _, _, first, last, _, _), end in zip(parts, ends):
        field[pl.ds(first, last - first)] = result[end - last + first : end]
    return fluxes


def turn(columns, result, at):
    block = jnp.swapaxes(columns, 0, 1)
    for half in range(result.shape[0]):
        result[half, :, at] = block[:, :, half * LANES : (half + 1) * LANES]


def pack(result, band_rows, bands, copies):
    halves, channels, count, _ = result.shape
    part = channels // 2
    total = bands.shape[0]
    lane = lax.broadcasted_iota(jnp.int32, (count, LANES), 1)
    start = jnp.int32(0)
    for b in range(total):
        half = start // LANES
        offset = start - half * LANES
        beyond = lax.rem(half + 1, halves)
        for v in range(2):
            packed = None
            for l in range(part):
                i = v * part + l
                window = jnp.where(lane >= offset, result[half, i], result[beyond, i])
                shift = lax.rem(LANES + l * CAP - offset, LANES)
                turned = pltpu.roll(window, shift, 1)
                packed = turned if l == 0 else jnp.where(lane >= l * CAP, turned, packed)
            bands[b, v] = packed
        start = start + band_rows[b]
        if (b + 1) * len(copies) % total == 0:
            copies[(b + 1) * len(copies) // total - 1].start()


def inner_kernel(band_rows, mine, field, along_x, along_y, down_y, sides, result, bands, ready, sems):
    groups, width, channels, rows = mine.shape
    for s in range(groups):
        spread_out(mine.at[s], pl.ds(s * width, width), field, along_x, along_y, down_y)
    span = groups * width
    for step in range(STEPS):
        last = step + 1
        behind = None
        for first in range(step + 1, span - 1 - step, BLOCK):
            last = min(first + BLOCK, span - 1 - step)
            piece = (field, along_x, along_y, down_y, first, last, behind, None)
            before, behind = advance([piece])[0]
            if first == step + 1:
                sides[0, step] = before
        sides[1, step] = behind
    for s in range(1, groups - 1):
        turn(field[pl.ds(s * width, width)], result, pl.ds((s - 1) * width, width))
    copy = pltpu.make_async_copy(ready, bands.at[:, :, pl.ds(0, span - 2 * width)], sems.at[0])
    pack(result, band_rows, ready, [copy])
    copy.wait()


def outer_kernel(groups, rows_far, low, high, *refs):
    inner, sides, inner_result, _, bands = refs[:4], *refs[4:8]
    strips = refs[8 : 8 + groups]
    ends, result, whole, ready, band_rows, sems = refs[8 + groups : 12 + groups], *refs[12 + groups :]
    rows_copy = pltpu.make_async_copy(rows_far, band_rows, sems.at[groups])
    rows_copy.start()
    width, _, rows = low.shape
    span = groups * width
    for side, (halo, own) in enumerate(((low, 0), (high, span - width))):
        arrays = [end.at[side] for end in ends]
        spread_out(halo, pl.ds(side * width, width), *arrays)
        for end, array in zip(arrays, inner):
            end[pl.ds((1 - side) * width, width)] = array[pl.ds(own, width)]
    for step in range(STEPS):
        pieces = []
        for side, first in enumerate((step + 1, width - 1 - step)):
            arrays = [end.at[side] for end in ends]
            faces = (sides[1, step], None) if side else (None, sides[0, step])
            pieces.append((*arrays, first, first + width, *faces))
        advance(pieces)
    field = ends[0]
    turn(field[0, pl.ds(width, width)], result, pl.ds(0, width))
    turn(field[1, pl.ds(0, width)], result, pl.ds(width, width))

    copies = []
    each = bands.shape[0] // groups
    for i in range(groups):
        near = pl.ds(i * each, each)
        target = bands.at[near, :, pl.ds(span - 2 * width, 2 * width)]
        copies.append(pltpu.make_async_copy(ready.at[near], target, sems.at[i]))
    rows_copy.wait()
    pack(result, band_rows, ready, copies)

    me = lax.rem(lax.axis_index("band"), groups)
    whole[:, :, pl.ds(width, span - 2 * width)] = inner_result[...]
    whole[:, :, pl.ds(0, width)] = result[:, :, pl.ds(0, width)]
    whole[:, :, pl.ds(span - width, width)] = result[:, :, pl.ds(width, width)]
    for k in range(groups):
        s = jnp.bitwise_xor(me, k)
        for half in range(rows // LANES):
            strips[k][:, :, half * LANES : (half + 1) * LANES] = whole[
                half, :, pl.ds(pl.multiple_of(s * width, width), width)
            ]
    for copy in copies:
        copy.wait()


def filtered(taps, v, l, levels, whole):
    total = whole[v, l]
    for tap in range(TAPS):
        other = l + tap - TAPS // 2
        if 0 <= other < levels:
            total = total + taps(tap, v, l) * whole[v, other]
    return total


def increment_kernel(groups, band_rows, weights, *refs):
    pieces, out, taps, keep, whole = refs[:groups], *refs[groups:]
    variables, levels = out.shape[:2]
    part = levels // groups
    me = lax.rem(lax.axis_index("band"), groups)
    for k in range(groups):
        near = pl.ds(jnp.bitwise_xor(me, k) * part, part)
        for v in range(variables):
            whole[v, near] = pieces[k][pl.ds(v * part, part)]
    for v in range(variables):
        for l in range(levels):
            out[v, l] = filtered(lambda a, b, c: weights[a, b, c], v, l, levels, whole)
            for tap in range(TAPS):
                taps[tap, v, l] = jnp.full(taps.shape[3:], weights[tap, v, l])
    row = lax.broadcasted_iota(jnp.int32, keep.shape, 0)
    keep[...] = (row < band_rows[lax.axis_index("band")]).astype(jnp.int32)


def band_kernel(groups, width, taps, keep, arrived, out, whole, ready, sems):
    variables, levels, height, _ = out.shape
    part = levels // groups
    count, _, span, _ = arrived.shape
    inside = span - 2 * width
    mine = keep[...] > 0
    copies = []
    for v in range(variables):
        for q in range(groups):
            blocks = []
            for s in range(q, count, groups):
                blocks += [arrived[s, v, inside : inside + width], arrived[s, v, :inside]]
                blocks += [arrived[s, v, inside + width :]]
            flat = jnp.transpose(jnp.concatenate(blocks, 0))
            for l in range(part):
                whole[v, q * part + l] = flat[l * height : (l + 1) * height]
    for v in range(variables):
        for l in range(levels):
            total = filtered(lambda a, b, c: taps[a, b, c], v, l, levels, whole)
            ready[v, l] = jnp.where(mine, total, 0.0)
            if (l + 1) % part == 0:
                near = pl.ds(l + 1 - part, part)
                i = len(copies)
                copies.append(
                    pltpu.make_async_copy(ready.at[v, near], out.at[v, near], sems.at[i])
                )
                copies[i].start()
    for copy in copies:
        copy.wait()


def shards(mesh_shape, background, scale_x, scale_y, filter_bands, band_rows):
    variables, levels, width, rows = background.shape
    count, blocks = mesh_shape["band"], mesh_shape["lon"]
    groups = math.isqrt(count)
    part = levels // groups
    channels = (variables + 2) * part
    f32 = jnp.float32

    def struct(*shape):
        return jax.ShapeDtypeStruct(shape, f32)

    parted = pl.pallas_call(
        regroup_kernel,
        out_shape=struct(groups, width, channels, rows),
        in_specs=[HBM] * 3,
        out_specs=VMEM,
        scratch_shapes=[pltpu.VMEM(a.shape, f32) for a in (background, scale_x, scale_y)]
        + [pltpu.SemaphoreType.DMA((groups, 3))],
        compiler_params=ROOM,
        name="regroup",
    )(*(pltpu.with_memory_space_constraint(a, pltpu.HBM) for a in (background, scale_x, scale_y)))
    weights = jnp.transpose(filter_bands, (1, 0, 2))
    near = [[g * groups + i for i in range(groups)] for g in range(count // groups)]
    mine = lax.all_to_all(
        parted, "band", split_axis=0, concat_axis=0, tiled=True, axis_index_groups=near
    )

    def shifted(by):
        total = count * blocks
        pairs = []
        for source in range(total):
            target = (source + by) % total
            pairs.append(
                (
                    source % count * blocks + source // count,
                    target % count * blocks + target // count,
                )
            )
        return pairs

    axes = ("band", "lon")
    low = lax.ppermute(mine[groups - 1], axes, shifted(groups))
    high = lax.ppermute(mine[0], axes, shifted(-groups))
    span = groups * width
    inside = span - 2 * width
    halves = rows // LANES
    both = variables * part
    inner = pl.pallas_call(
        inner_kernel,
        out_shape=[struct(span, both, rows)] * 4
        + [
            struct(2, STEPS, both, rows),
            struct(halves, both, inside, LANES),
            struct(count, variables, span, LANES),
        ],
        in_specs=[SMEM, VMEM],
        out_specs=[VMEM] * 6 + [HBM],
        scratch_shapes=[
            pltpu.VMEM((count, variables, inside, LANES), f32),
            pltpu.SemaphoreType.DMA((1,)),
        ],
        compiler_params=ROOM,
        cost_estimate=pl.CostEstimate(
            flops=20 * STEPS * span * both * rows, bytes_accessed=2**20, transcendentals=0
        ),
        name="inner",
    )(band_rows, mine)
    outs = pl.pallas_call(
        functools.partial(outer_kernel, groups),
        out_shape=[struct(count, variables, span, LANES)] + [struct(both, width, rows)] * groups,
        in_specs=[HBM] + [VMEM] * 8 + [HBM],
        out_specs=[HBM] + [VMEM] * groups,
        input_output_aliases={9: 0},
        scratch_shapes=[pltpu.VMEM((2, 2 * width, both, rows), f32)] * 4
        + [
            pltpu.VMEM((halves, both, 2 * width, LANES), f32),
            pltpu.VMEM((halves, both, span, LANES), f32),
            pltpu.VMEM((count, variables, 2 * width, LANES), f32),
            pltpu.SMEM(band_rows.shape, band_rows.dtype),
            pltpu.SemaphoreType.DMA((groups + 1,)),
        ],
        compiler_params=ROOM,
        name="outer",
    )(band_rows, low, high, *inner)
    bands, strips = outs[0], outs[1:]
    arrived = lax.all_to_all(bands, "band", split_axis=0, concat_axis=0, tiled=True)
    pieces = [strips[0]] + [
        lax.ppermute(strips[k], "band", [(i, i ^ k) for i in range(count)])
        for k in range(1, groups)
    ]
    increment, taps, keep = pl.pallas_call(
        functools.partial(increment_kernel, groups),
        out_shape=[
            struct(*background.shape),
            struct(TAPS, variables, levels, 1, count * width),
            jax.ShapeDtypeStruct((CAP, count * width), jnp.int32),
        ],
        in_specs=[SMEM, SMEM] + [VMEM] * groups,
        out_specs=[VMEM] * 3,
        scratch_shapes=[pltpu.VMEM((variables, levels, width, rows), f32)],
        compiler_params=ROOM,
        name="increment",
    )(band_rows, weights, *pieces)
    band_field = pl.pallas_call(
        functools.partial(band_kernel, groups, width),
        out_shape=struct(variables, levels, CAP, count * width),
        in_specs=[VMEM] * 3,
        out_specs=HBM,
        scratch_shapes=[pltpu.VMEM((variables, levels, CAP, count * width), f32)] * 2
        + [pltpu.SemaphoreType.DMA((variables * groups,))],
        compiler_params=ROOM,
        name="bands",
    )(taps, keep, arrived)
    return increment, band_field


def solution(mesh):
    in_specs = (
        P(None, None, ("lon", "band"), None),
        P(None, ("lon", "band"), None),
        P(None, ("lon", "band"), None),
        P(),
        P(),
    )
    out_specs = (P(None, None, ("lon", "band"), None), P(None, None, "band", "lon"))
    return jax.shard_map(
        functools.partial(shards, dict(mesh.shape)),
        mesh=mesh,
        in_specs=in_specs,
        out_specs=out_specs,
        check_vma=False,
    )
```

```python
import functools
import math

import jax
import jax.numpy as jnp
from jax import lax
from jax.experimental import pallas as pl
from jax.experimental.pallas import tpu as pltpu
from jax.sharding import PartitionSpec as P

STEPS = 8
CAP = 32
LANES = 128
TAPS = 5
BLOCK = 16
VMEM = pl.BlockSpec(memory_space=pltpu.VMEM)
SMEM = pl.BlockSpec(memory_space=pltpu.SMEM)
HBM = pl.BlockSpec(memory_space=pltpu.HBM)
ROOM = pltpu.CompilerParams(vmem_limit_bytes=8 * 2**20)


def member(groups):
    return lax.rem(lax.axis_index("band"), groups)


def regroup_kernel(background, scale_x, scale_y, *refs):
    *pieces, field, along_x, along_y, sems = refs
    variables, levels = background.shape[:2]
    part = levels // len(pieces)
    me = member(len(pieces))
    parts, copies = [], []
    for k in range(len(pieces)):
        near = pl.ds(jnp.bitwise_xor(me, k) * part, part)
        parts.append(near)
        copies.append(
            [
                pltpu.make_async_copy(background.at[:, near], field.at[:, near], sems.at[k, 0]),
                pltpu.make_async_copy(scale_x.at[near], along_x.at[near], sems.at[k, 1]),
                pltpu.make_async_copy(scale_y.at[near], along_y.at[near], sems.at[k, 2]),
            ]
        )
        for copy in copies[k]:
            copy.start()
    for near, piece, each in zip(parts, pieces, copies):
        for copy in each:
            copy.wait()
        sources = [field[v, near] for v in range(variables)]
        sources += [along_x[near], along_y[near]]
        piece[...] = jnp.swapaxes(jnp.concatenate(sources, 0), 0, 1)


def edges_kernel(*refs):
    *pieces, first, last = refs
    groups = len(pieces)
    me = member(groups)
    for k, piece in enumerate(pieces):

        @pl.when(me == k)
        def _(piece=piece):
            first[...] = piece[...]

        @pl.when(me == groups - 1 - k)
        def _(piece=piece):
            last[...] = piece[...]


def spread_out(source, near, field, along_x, along_y, down_y):
    _, channels, rows = source.shape
    part = channels // 4
    pairs = 2 * part
    upper = lax.broadcasted_iota(jnp.int32, (1, pairs, rows), 1) < part
    inside = lax.broadcasted_iota(jnp.int32, (1, pairs, rows), 2) < rows - 1
    field[near] = source[:, :pairs]
    coefs = source[:, pairs:]
    swapped = pltpu.roll(coefs, part, 1)
    along_x[near] = jnp.where(upper, coefs, swapped)
    flow_y = jnp.where(inside, jnp.where(upper, swapped, coefs), 0.0)
    along_y[near] = flow_y
    down_y[near] = pltpu.roll(flow_y, 1, 2)


def advance(parts):
    joined, fluxes, ends = [], [], []
    for field, along_x, along_y, down_y, first, last, before, behind in parts:
        near = pl.ds(first, last - first)
        here = field[near]
        inner = along_x[pl.ds(first, last - first - 1)] * (here[1:] - here[:-1])
        if before is None:
            before = along_x[first - 1] * (here[0] - field[first - 1])
        if behind is None:
            behind = along_x[last - 1] * (field[last] - here[-1])
        fluxes.append((before, behind))
        entering = jnp.concatenate([before[None], inner], 0)
        leaving = jnp.concatenate([inner, behind[None]], 0)
        joined.append((here, leaving, entering, along_y[near], down_y[near]))
        ends.append(sum(ends[-1:]) + last - first)
    here, leaving, entering, up, down = (jnp.concatenate(each, 0) for each in zip(*joined))
    rows = here.shape[-1]
    flux_y = up * (pltpu.roll(here, rows - 1, 2) - here)
    under = down * (here - pltpu.roll(here, 1, 2))
    result = here + leaving - entering + flux_y - under
    for (field, _, _, _, first, last, _, _), end in zip(parts, ends):
        field[pl.ds(first, last - first)] = result[end - last + first : end]
    return fluxes


def turn(columns, result, at):
    block = jnp.swapaxes(columns, 0, 1)
    for half in range(result.shape[0]):
        result[half, :, at] = block[:, :, half * LANES : (half + 1) * LANES]


def pack(result, band_rows, bands, copies):
    halves, channels, count, _ = result.shape
    part = channels // 2
    total = bands.shape[0]
    lane = lax.broadcasted_iota(jnp.int32, (count, LANES), 1)
    start = jnp.int32(0)
    for b in range(total):
        half = start // LANES
        offset = start - half * LANES
        beyond = lax.rem(half + 1, halves)
        for v in range(2):
            packed = None
            for l in range(part):
                i = v * part + l
                window = jnp.where(lane >= offset, result[half, i], result[beyond, i])
                shift = lax.rem(LANES + l * CAP - offset, LANES)
                turned = pltpu.roll(window, shift, 1)
                packed = turned if l == 0 else jnp.where(lane >= l * CAP, turned, packed)
            bands[b, v] = packed
        start = start + band_rows[b]
        if (b + 1) * len(copies) % total == 0:
            copies[(b + 1) * len(copies) // total - 1].start()


def inner_kernel(groups, band_rows, *refs):
    pieces, field, along_x, along_y, down_y = refs[:groups], *refs[groups : groups + 4]
    sides, result, bands, ready, sems = refs[groups + 4 :]
    width = pieces[0].shape[0]
    me = member(groups)
    for k, piece in enumerate(pieces):
        near = pl.ds(jnp.bitwise_xor(me, k) * width, width)
        spread_out(piece, near, field, along_x, along_y, down_y)
    span = groups * width
    for step in range(STEPS):
        last = step + 1
        behind = None
        for first in range(step + 1, span - 1 - step, BLOCK):
            last = min(first + BLOCK, span - 1 - step)
            piece = (field, along_x, along_y, down_y, first, last, behind, None)
            before, behind = advance([piece])[0]
            if first == step + 1:
                sides[0, step] = before
        sides[1, step] = behind
    for s in range(1, groups - 1):
        turn(field[pl.ds(s * width, width)], result, pl.ds((s - 1) * width, width))
    copy = pltpu.make_async_copy(ready, bands.at[:, :, pl.ds(0, span - 2 * width)], sems.at[0])
    pack(result, band_rows, ready, [copy])
    copy.wait()


def outer_kernel(groups, rows_far, low, high, *refs):
    inner, sides, inner_result, _, bands = refs[:4], *refs[4:8]
    strips = refs[8 : 8 + groups]
    ends, result, whole, ready, band_rows, sems = refs[8 + groups : 12 + groups], *refs[12 + groups :]
    rows_copy = pltpu.make_async_copy(rows_far, band_rows, sems.at[groups])
    rows_copy.start()
    width, _, rows = low.shape
    span = groups * width
    for side, (halo, own) in enumerate(((low, 0), (high, span - width))):
        arrays = [end.at[side] for end in ends]
        spread_out(halo, pl.ds(side * width, width), *arrays)
        for end, array in zip(arrays, inner):
            end[pl.ds((1 - side) * width, width)] = array[pl.ds(own, width)]
    for step in range(STEPS):
        pieces = []
        for side, first in enumerate((step + 1, width - 1 - step)):
            arrays = [end.at[side] for end in ends]
            faces = (sides[1, step], None) if side else (None, sides[0, step])
            pieces.append((*arrays, first, first + width, *faces))
        advance(pieces)
    field = ends[0]
    turn(field[0, pl.ds(width, width)], result, pl.ds(0, width))
    turn(field[1, pl.ds(0, width)], result, pl.ds(width, width))

    copies = []
    each = bands.shape[0] // groups
    for i in range(groups):
        near = pl.ds(i * each, each)
        target = bands.at[near, :, pl.ds(span - 2 * width, 2 * width)]
        copies.append(pltpu.make_async_copy(ready.at[near], target, sems.at[i]))
    rows_copy.wait()
    pack(result, band_rows, ready, copies)

    me = member(groups)
    whole[:, :, pl.ds(width, span - 2 * width)] = inner_result[...]
    whole[:, :, pl.ds(0, width)] = result[:, :, pl.ds(0, width)]
    whole[:, :, pl.ds(span - width, width)] = result[:, :, pl.ds(width, width)]
    for k in range(groups):
        s = jnp.bitwise_xor(me, k)
        for half in range(rows // LANES):
            strips[k][:, :, half * LANES : (half + 1) * LANES] = whole[
                half, :, pl.ds(pl.multiple_of(s * width, width), width)
            ]
    for copy in copies:
        copy.wait()


def filtered(taps, v, l, levels, whole):
    total = whole[v, l]
    for tap in range(TAPS):
        other = l + tap - TAPS // 2
        if 0 <= other < levels:
            total = total + taps(tap, v, l) * whole[v, other]
    return total


def increment_kernel(groups, band_rows, weights, *refs):
    pieces, out, taps, keep, whole = refs[:groups], *refs[groups:]
    variables, levels = out.shape[:2]
    part = levels // groups
    me = member(groups)
    for k in range(groups):
        near = pl.ds(jnp.bitwise_xor(me, k) * part, part)
        for v in range(variables):
            whole[v, near] = pieces[k][pl.ds(v * part, part)]
    for v in range(variables):
        for l in range(levels):
            out[v, l] = filtered(lambda a, b, c: weights[a, b, c], v, l, levels, whole)
            for tap in range(TAPS):
                taps[tap, v, l] = jnp.full(taps.shape[3:], weights[tap, v, l])
    row = lax.broadcasted_iota(jnp.int32, keep.shape, 0)
    keep[...] = (row < band_rows[lax.axis_index("band")]).astype(jnp.int32)


def band_kernel(groups, width, taps, keep, arrived, out, whole, ready, sems):
    variables, levels, height, _ = out.shape
    part = levels // groups
    count, _, span, _ = arrived.shape
    inside = span - 2 * width
    mine = keep[...] > 0
    copies = []
    for v in range(variables):
        for q in range(groups):
            blocks = []
            for s in range(q, count, groups):
                blocks += [arrived[s, v, inside : inside + width], arrived[s, v, :inside]]
                blocks += [arrived[s, v, inside + width :]]
            flat = jnp.transpose(jnp.concatenate(blocks, 0))
            for l in range(part):
                whole[v, q * part + l] = flat[l * height : (l + 1) * height]
    for v in range(variables):
        for l in range(levels):
            total = filtered(lambda a, b, c: taps[a, b, c], v, l, levels, whole)
            ready[v, l] = jnp.where(mine, total, 0.0)
            if (l + 1) % part == 0:
                near = pl.ds(l + 1 - part, part)
                i = len(copies)
                copies.append(
                    pltpu.make_async_copy(ready.at[v, near], out.at[v, near], sems.at[i])
                )
                copies[i].start()
    for copy in copies:
        copy.wait()


def shards(mesh_shape, background, scale_x, scale_y, filter_bands, band_rows):
    variables, levels, width, rows = background.shape
    count, blocks = mesh_shape["band"], mesh_shape["lon"]
    groups = math.isqrt(count)
    part = levels // groups
    channels = (variables + 2) * part
    f32 = jnp.float32

    def struct(*shape):
        return jax.ShapeDtypeStruct(shape, f32)

    piece = struct(width, channels, rows)
    parted = pl.pallas_call(
        regroup_kernel,
        out_shape=[piece] * groups,
        in_specs=[HBM] * 3,
        out_specs=[VMEM] * groups,
        scratch_shapes=[pltpu.VMEM(a.shape, f32) for a in (background, scale_x, scale_y)]
        + [pltpu.SemaphoreType.DMA((groups, 3))],
        compiler_params=ROOM,
        name="regroup",
    )(*(pltpu.with_memory_space_constraint(a, pltpu.HBM) for a in (background, scale_x, scale_y)))
    weights = jnp.transpose(filter_bands, (1, 0, 2))

    def exchanged(pieces):
        return [pieces[0]] + [
            lax.ppermute(pieces[k], "band", [(i, i ^ k) for i in range(count)])
            for k in range(1, groups)
        ]

    mine = exchanged(parted)
    first, last = pl.pallas_call(
        edges_kernel,
        out_shape=[piece] * 2,
        in_specs=[VMEM] * groups,
        out_specs=[VMEM] * 2,
        compiler_params=ROOM,
        name="edges",
    )(*mine)

    def shifted(by):
        total = count * blocks
        pairs = []
        for source in range(total):
            target = (source + by) % total
            pairs.append(
                (
                    source % count * blocks + source // count,
                    target % count * blocks + target // count,
                )
            )
        return pairs

    axes = ("band", "lon")
    low = lax.ppermute(last, axes, shifted(groups))
    high = lax.ppermute(first, axes, shifted(-groups))
    span = groups * width
    inside = span - 2 * width
    halves = rows // LANES
    both = variables * part
    inner = pl.pallas_call(
        functools.partial(inner_kernel, groups),
        out_shape=[struct(span, both, rows)] * 4
        + [
            struct(2, STEPS, both, rows),
            struct(halves, both, inside, LANES),
            struct(count, variables, span, LANES),
        ],
        in_specs=[SMEM] + [VMEM] * groups,
        out_specs=[VMEM] * 6 + [HBM],
        scratch_shapes=[
            pltpu.VMEM((count, variables, inside, LANES), f32),
            pltpu.SemaphoreType.DMA((1,)),
        ],
        compiler_params=ROOM,
        cost_estimate=pl.CostEstimate(
            flops=20 * STEPS * span * both * rows, bytes_accessed=2**20, transcendentals=0
        ),
        name="inner",
    )(band_rows, *mine)
    outs = pl.pallas_call(
        functools.partial(outer_kernel, groups),
        out_shape=[struct(count, variables, span, LANES)] + [struct(both, width, rows)] * groups,
        in_specs=[HBM] + [VMEM] * 8 + [HBM],
        out_specs=[HBM] + [VMEM] * groups,
        input_output_aliases={9: 0},
        scratch_shapes=[pltpu.VMEM((2, 2 * width, both, rows), f32)] * 4
        + [
            pltpu.VMEM((halves, both, 2 * width, LANES), f32),
            pltpu.VMEM((halves, both, span, LANES), f32),
            pltpu.VMEM((count, variables, 2 * width, LANES), f32),
            pltpu.SMEM(band_rows.shape, band_rows.dtype),
            pltpu.SemaphoreType.DMA((groups + 1,)),
        ],
        compiler_params=ROOM,
        name="outer",
    )(band_rows, low, high, *inner)
    bands, strips = outs[0], outs[1:]
    arrived = lax.all_to_all(bands, "band", split_axis=0, concat_axis=0, tiled=True)
    pieces = exchanged(strips)
    increment, taps, keep = pl.pallas_call(
        functools.partial(increment_kernel, groups),
        out_shape=[
            struct(*background.shape),
            struct(TAPS, variables, levels, 1, count * width),
            jax.ShapeDtypeStruct((CAP, count * width), jnp.int32),
        ],
        in_specs=[SMEM, SMEM] + [VMEM] * groups,
        out_specs=[VMEM] * 3,
        scratch_shapes=[pltpu.VMEM((variables, levels, width, rows), f32)],
        compiler_params=ROOM,
        name="increment",
    )(band_rows, weights, *pieces)
    band_field = pl.pallas_call(
        functools.partial(band_kernel, groups, width),
        out_shape=struct(variables, levels, CAP, count * width),
        in_specs=[VMEM] * 3,
        out_specs=HBM,
        scratch_shapes=[pltpu.VMEM((variables, levels, CAP, count * width), f32)] * 2
        + [pltpu.SemaphoreType.DMA((variables * groups,))],
        compiler_params=ROOM,
        name="bands",
    )(taps, keep, arrived)
    return increment, band_field


def solution(mesh):
    in_specs = (
        P(None, None, ("lon", "band"), None),
        P(None, ("lon", "band"), None),
        P(None, ("lon", "band"), None),
        P(),
        P(),
    )
    out_specs = (P(None, None, ("lon", "band"), None), P(None, None, "band", "lon"))
    return jax.shard_map(
        functools.partial(shards, dict(mesh.shape)),
        mesh=mesh,
        in_specs=in_specs,
        out_specs=out_specs,
        check_vma=False,
    )
```

```python
import functools
import math

import jax
import jax.numpy as jnp
from jax import lax
from jax.experimental import pallas as pl
from jax.experimental.pallas import tpu as pltpu
from jax.sharding import PartitionSpec as P

STEPS = 8
CAP = 32
LANES = 128
TAPS = 5
BLOCK = 16
VMEM = pl.BlockSpec(memory_space=pltpu.VMEM)
SMEM = pl.BlockSpec(memory_space=pltpu.SMEM)
HBM = pl.BlockSpec(memory_space=pltpu.HBM)
ROOM = pltpu.CompilerParams(vmem_limit_bytes=8 * 2**20)


def member(groups):
    return lax.rem(lax.axis_index("band"), groups)


def regroup_kernel(background, scale_x, scale_y, *refs):
    *pieces, field, along_x, along_y, sems = refs
    variables, levels = background.shape[:2]
    part = levels // len(pieces)
    me = member(len(pieces))
    parts, copies = [], []
    for k in range(len(pieces)):
        near = pl.ds(jnp.bitwise_xor(me, k) * part, part)
        parts.append(near)
        copies.append(
            [
                pltpu.make_async_copy(background.at[:, near], field.at[:, near], sems.at[k, 0]),
                pltpu.make_async_copy(scale_x.at[near], along_x.at[near], sems.at[k, 1]),
                pltpu.make_async_copy(scale_y.at[near], along_y.at[near], sems.at[k, 2]),
            ]
        )
        for copy in copies[k]:
            copy.start()
    for near, piece, each in zip(parts, pieces, copies):
        for copy in each:
            copy.wait()
        sources = [field[v, near] for v in range(variables)]
        sources += [along_x[near], along_y[near]]
        piece[...] = jnp.swapaxes(jnp.concatenate(sources, 0), 0, 1)


def edges_kernel(*refs):
    *pieces, first, last = refs
    groups = len(pieces)
    me = member(groups)
    for k, piece in enumerate(pieces):

        @pl.when(me == k)
        def _(piece=piece):
            first[...] = piece[...]

        @pl.when(me == groups - 1 - k)
        def _(piece=piece):
            last[...] = piece[...]


def spread_out(source, near, field, along_x, along_y, down_y):
    _, channels, rows = source.shape
    part = channels // 4
    pairs = 2 * part
    upper = lax.broadcasted_iota(jnp.int32, (1, pairs, rows), 1) < part
    inside = lax.broadcasted_iota(jnp.int32, (1, pairs, rows), 2) < rows - 1
    field[near] = source[:, :pairs]
    coefs = source[:, pairs:]
    swapped = pltpu.roll(coefs, part, 1)
    along_x[near] = jnp.where(upper, coefs, swapped)
    flow_y = jnp.where(inside, jnp.where(upper, swapped, coefs), 0.0)
    along_y[near] = flow_y
    down_y[near] = pltpu.roll(flow_y, 1, 2)


def advance(parts):
    joined, fluxes, ends = [], [], []
    for field, along_x, along_y, down_y, first, last, before, behind in parts:
        near = pl.ds(first, last - first)
        here = field[near]
        inner = along_x[pl.ds(first, last - first - 1)] * (here[1:] - here[:-1])
        if before is None:
            before = along_x[first - 1] * (here[0] - field[first - 1])
        if behind is None:
            behind = along_x[last - 1] * (field[last] - here[-1])
        fluxes.append((before, behind))
        entering = jnp.concatenate([before[None], inner], 0)
        leaving = jnp.concatenate([inner, behind[None]], 0)
        joined.append((here, leaving, entering, along_y[near], down_y[near]))
        ends.append(sum(ends[-1:]) + last - first)
    here, leaving, entering, up, down = (jnp.concatenate(each, 0) for each in zip(*joined))
    rows = here.shape[-1]
    flux_y = up * (pltpu.roll(here, rows - 1, 2) - here)
    under = down * (here - pltpu.roll(here, 1, 2))
    result = here + leaving - entering + flux_y - under
    for (field, _, _, _, first, last, _, _), end in zip(parts, ends):
        field[pl.ds(first, last - first)] = result[end - last + first : end]
    return fluxes


def turn(columns, result, at):
    block = jnp.swapaxes(columns, 0, 1)
    for half in range(result.shape[0]):
        result[half, :, at] = block[:, :, half * LANES : (half + 1) * LANES]


def pack(result, band_rows, bands, copies):
    halves, channels, count, _ = result.shape
    part = channels // 2
    total = bands.shape[0]
    lane = lax.broadcasted_iota(jnp.int32, (count, LANES), 1)
    start = jnp.int32(0)
    for b in range(total):
        half = start // LANES
        offset = start - half * LANES
        beyond = lax.rem(half + 1, halves)
        for v in range(2):
            packed = None
            for l in range(part):
                i = v * part + l
                window = jnp.where(lane >= offset, result[half, i], result[beyond, i])
                shift = lax.rem(LANES + l * CAP - offset, LANES)
                turned = pltpu.roll(window, shift, 1)
                packed = turned if l == 0 else jnp.where(lane >= l * CAP, turned, packed)
            bands[b, v] = packed
        start = start + band_rows[b]
        if (b + 1) * len(copies) % total == 0:
            copies[(b + 1) * len(copies) // total - 1].start()


def inner_kernel(groups, band_rows, *refs):
    pieces, field, along_x, along_y, down_y = refs[:groups], *refs[groups : groups + 4]
    sides, result, bands, ready, sems = refs[groups + 4 :]
    width = pieces[0].shape[0]
    me = member(groups)
    for k, piece in enumerate(pieces):
        near = pl.ds(jnp.bitwise_xor(me, k) * width, width)
        spread_out(piece, near, field, along_x, along_y, down_y)
    span = groups * width
    for step in range(STEPS):
        last = step + 1
        behind = None
        for first in range(step + 1, span - 1 - step, BLOCK):
            last = min(first + BLOCK, span - 1 - step)
            piece = (field, along_x, along_y, down_y, first, last, behind, None)
            before, behind = advance([piece])[0]
            if first == step + 1:
                sides[0, step] = before
        sides[1, step] = behind
    for s in range(1, groups - 1):
        turn(field[pl.ds(s * width, width)], result, pl.ds((s - 1) * width, width))
    copy = pltpu.make_async_copy(ready, bands.at[:, :, pl.ds(0, span - 2 * width)], sems.at[0])
    pack(result, band_rows, ready, [copy])
    copy.wait()


def end_kernel(groups, side, rows_far, halo, *refs):
    inner, sides, _, bands, result = refs[:4], *refs[4:8]
    end, ready, band_rows, sems = refs[8:12], *refs[12:]
    rows_copy = pltpu.make_async_copy(rows_far, band_rows, sems.at[groups])
    rows_copy.start()
    width = halo.shape[0]
    span = groups * width
    spread_out(halo, pl.ds(side * width, width), *end)
    for here, array in zip(end, inner):
        here[pl.ds((1 - side) * width, width)] = array[pl.ds(side * (span - width), width)]
    for step in range(STEPS):
        first = width - 1 - step if side else step + 1
        faces = (sides[1, step], None) if side else (None, sides[0, step])
        advance([(*end, first, first + width, *faces)])
    turn(end[0][pl.ds((1 - side) * width, width)], result, pl.ds(0, width))

    copies = []
    each = bands.shape[0] // groups
    for i in range(groups):
        near = pl.ds(i * each, each)
        target = bands.at[near, :, pl.ds(span - (2 - side) * width, width)]
        copies.append(pltpu.make_async_copy(ready.at[near], target, sems.at[i]))
    rows_copy.wait()
    pack(result, band_rows, ready, copies)
    for copy in copies:
        copy.wait()


def strips_kernel(groups, low, inner, high, *refs):
    strips, whole = refs[:groups], refs[groups]
    halves, _, width, _ = low.shape
    span = groups * width
    me = member(groups)
    whole[:, :, pl.ds(0, width)] = low[...]
    whole[:, :, pl.ds(width, span - 2 * width)] = inner[...]
    whole[:, :, pl.ds(span - width, width)] = high[...]
    for k in range(groups):
        s = jnp.bitwise_xor(me, k)
        for half in range(halves):
            strips[k][:, :, half * LANES : (half + 1) * LANES] = whole[
                half, :, pl.ds(pl.multiple_of(s * width, width), width)
            ]


def filtered(taps, v, l, levels, whole):
    total = whole[v, l]
    for tap in range(TAPS):
        other = l + tap - TAPS // 2
        if 0 <= other < levels:
            total = total + taps(tap, v, l) * whole[v, other]
    return total


def increment_kernel(groups, band_rows, weights, *refs):
    pieces, out, taps, keep, whole = refs[:groups], *refs[groups:]
    variables, levels = out.shape[:2]
    part = levels // groups
    me = member(groups)
    for k in range(groups):
        near = pl.ds(jnp.bitwise_xor(me, k) * part, part)
        for v in range(variables):
            whole[v, near] = pieces[k][pl.ds(v * part, part)]
    for v in range(variables):
        for l in range(levels):
            out[v, l] = filtered(lambda a, b, c: weights[a, b, c], v, l, levels, whole)
            for tap in range(TAPS):
                taps[tap, v, l] = jnp.full(taps.shape[3:], weights[tap, v, l])
    row = lax.broadcasted_iota(jnp.int32, keep.shape, 0)
    keep[...] = (row < band_rows[lax.axis_index("band")]).astype(jnp.int32)


def band_kernel(groups, width, taps, keep, arrived, out, whole, ready, sems):
    variables, levels, height, _ = out.shape
    part = levels // groups
    count, _, span, _ = arrived.shape
    inside = span - 2 * width
    mine = keep[...] > 0
    copies = []
    for v in range(variables):
        for q in range(groups):
            blocks = []
            for s in range(q, count, groups):
                blocks += [arrived[s, v, inside : inside + width], arrived[s, v, :inside]]
                blocks += [arrived[s, v, inside + width :]]
            flat = jnp.transpose(jnp.concatenate(blocks, 0))
            for l in range(part):
                whole[v, q * part + l] = flat[l * height : (l + 1) * height]
    for v in range(variables):
        for l in range(levels):
            total = filtered(lambda a, b, c: taps[a, b, c], v, l, levels, whole)
            ready[v, l] = jnp.where(mine, total, 0.0)
            if (l + 1) % part == 0:
                near = pl.ds(l + 1 - part, part)
                i = len(copies)
                copies.append(
                    pltpu.make_async_copy(ready.at[v, near], out.at[v, near], sems.at[i])
                )
                copies[i].start()
    for copy in copies:
        copy.wait()


def shards(mesh_shape, background, scale_x, scale_y, filter_bands, band_rows):
    variables, levels, width, rows = background.shape
    count, blocks = mesh_shape["band"], mesh_shape["lon"]
    groups = math.isqrt(count)
    part = levels // groups
    channels = (variables + 2) * part
    f32 = jnp.float32

    def struct(*shape):
        return jax.ShapeDtypeStruct(shape, f32)

    piece = struct(width, channels, rows)
    parted = pl.pallas_call(
        regroup_kernel,
        out_shape=[piece] * groups,
        in_specs=[HBM] * 3,
        out_specs=[VMEM] * groups,
        scratch_shapes=[pltpu.VMEM(a.shape, f32) for a in (background, scale_x, scale_y)]
        + [pltpu.SemaphoreType.DMA((groups, 3))],
        compiler_params=ROOM,
        name="regroup",
    )(*(pltpu.with_memory_space_constraint(a, pltpu.HBM) for a in (background, scale_x, scale_y)))
    weights = jnp.transpose(filter_bands, (1, 0, 2))

    def exchanged(pieces):
        return [pieces[0]] + [
            lax.ppermute(pieces[k], "band", [(i, i ^ k) for i in range(count)])
            for k in range(1, groups)
        ]

    mine = exchanged(parted)
    first, last = pl.pallas_call(
        edges_kernel,
        out_shape=[piece] * 2,
        in_specs=[VMEM] * groups,
        out_specs=[VMEM] * 2,
        compiler_params=ROOM,
        name="edges",
    )(*mine)

    def shifted(by):
        total = count * blocks
        pairs = []
        for source in range(total):
            target = (source + by) % total
            pairs.append(
                (
                    source % count * blocks + source // count,
                    target % count * blocks + target // count,
                )
            )
        return pairs

    axes = ("band", "lon")
    low = lax.ppermute(last, axes, shifted(groups))
    high = lax.ppermute(first, axes, shifted(-groups))
    span = groups * width
    inside = span - 2 * width
    halves = rows // LANES
    both = variables * part
    inner = pl.pallas_call(
        functools.partial(inner_kernel, groups),
        out_shape=[struct(span, both, rows)] * 4
        + [
            struct(2, STEPS, both, rows),
            struct(halves, both, inside, LANES),
            struct(count, variables, span, LANES),
        ],
        in_specs=[SMEM] + [VMEM] * groups,
        out_specs=[VMEM] * 6 + [HBM],
        scratch_shapes=[
            pltpu.VMEM((count, variables, inside, LANES), f32),
            pltpu.SemaphoreType.DMA((1,)),
        ],
        compiler_params=ROOM,
        cost_estimate=pl.CostEstimate(
            flops=20 * STEPS * span * both * rows, bytes_accessed=2**20, transcendentals=0
        ),
        name="inner",
    )(band_rows, *mine)
    *arrays, inner_result, bands = inner

    def finished(side, halo, bands):
        return pl.pallas_call(
            functools.partial(end_kernel, groups, side),
            out_shape=[
                struct(count, variables, span, LANES),
                struct(halves, both, width, LANES),
            ],
            in_specs=[HBM] + [VMEM] * 6 + [HBM],
            out_specs=[HBM, VMEM],
            input_output_aliases={7: 0},
            scratch_shapes=[pltpu.VMEM((2 * width, both, rows), f32)] * 4
            + [
                pltpu.VMEM((count, variables, width, LANES), f32),
                pltpu.SMEM(band_rows.shape, band_rows.dtype),
                pltpu.SemaphoreType.DMA((groups + 1,)),
            ],
            compiler_params=ROOM,
            name="high_end" if side else "low_end",
        )(band_rows, halo, *arrays, bands)

    bands, low_result = finished(0, low, bands)
    bands, high_result = finished(1, high, bands)
    strips = pl.pallas_call(
        functools.partial(strips_kernel, groups),
        out_shape=[struct(both, width, rows)] * groups,
        in_specs=[VMEM] * 3,
        out_specs=[VMEM] * groups,
        scratch_shapes=[pltpu.VMEM((halves, both, span, LANES), f32)],
        compiler_params=ROOM,
        name="strips",
    )(low_result, inner_result, high_result)
    arrived = lax.all_to_all(bands, "band", split_axis=0, concat_axis=0, tiled=True)
    pieces = exchanged(strips)
    increment, taps, keep = pl.pallas_call(
        functools.partial(increment_kernel, groups),
        out_shape=[
            struct(*background.shape),
            struct(TAPS, variables, levels, 1, count * width),
            jax.ShapeDtypeStruct((CAP, count * width), jnp.int32),
        ],
        in_specs=[SMEM, SMEM] + [VMEM] * groups,
        out_specs=[VMEM] * 3,
        scratch_shapes=[pltpu.VMEM((variables, levels, width, rows), f32)],
        compiler_params=ROOM,
        name="increment",
    )(band_rows, weights, *pieces)
    band_field = pl.pallas_call(
        functools.partial(band_kernel, groups, width),
        out_shape=struct(variables, levels, CAP, count * width),
        in_specs=[VMEM] * 3,
        out_specs=HBM,
        scratch_shapes=[pltpu.VMEM((variables, levels, CAP, count * width), f32)] * 2
        + [pltpu.SemaphoreType.DMA((variables * groups,))],
        compiler_params=ROOM,
        name="bands",
    )(taps, keep, arrived)
    return increment, band_field


def solution(mesh):
    in_specs = (
        P(None, None, ("lon", "band"), None),
        P(None, ("lon", "band"), None),
        P(None, ("lon", "band"), None),
        P(),
        P(),
    )
    out_specs = (P(None, None, ("lon", "band"), None), P(None, None, "band", "lon"))
    return jax.shard_map(
        functools.partial(shards, dict(mesh.shape)),
        mesh=mesh,
        in_specs=in_specs,
        out_specs=out_specs,
        check_vma=False,
    )
```

```python
import functools
import math

import jax
import jax.numpy as jnp
from jax import lax
from jax.experimental import pallas as pl
from jax.experimental.pallas import tpu as pltpu
from jax.sharding import PartitionSpec as P

STEPS = 8
CAP = 32
LANES = 128
TAPS = 5
BLOCK = 16
VMEM = pl.BlockSpec(memory_space=pltpu.VMEM)
SMEM = pl.BlockSpec(memory_space=pltpu.SMEM)
HBM = pl.BlockSpec(memory_space=pltpu.HBM)
ROOM = pltpu.CompilerParams(vmem_limit_bytes=8 * 2**20)


def member(groups):
    return lax.rem(lax.axis_index("band"), groups)


def regroup_kernel(background, scale_x, scale_y, *refs):
    *pieces, field, along_x, along_y, sems = refs
    variables, levels = background.shape[:2]
    part = levels // len(pieces)
    me = member(len(pieces))
    parts, copies = [], []
    for k in range(len(pieces)):
        near = pl.ds(jnp.bitwise_xor(me, k) * part, part)
        parts.append(near)
        copies.append(
            [
                pltpu.make_async_copy(background.at[:, near], field.at[:, near], sems.at[k, 0]),
                pltpu.make_async_copy(scale_x.at[near], along_x.at[near], sems.at[k, 1]),
                pltpu.make_async_copy(scale_y.at[near], along_y.at[near], sems.at[k, 2]),
            ]
        )
        for copy in copies[k]:
            copy.start()
    for near, piece, each in zip(parts, pieces, copies):
        for copy in each:
            copy.wait()
        sources = [field[v, near] for v in range(variables)]
        sources += [along_x[near], along_y[near]]
        piece[...] = jnp.swapaxes(jnp.concatenate(sources, 0), 0, 1)


def edges_kernel(*refs):
    *pieces, first, last = refs
    groups = len(pieces)
    me = member(groups)
    for k, piece in enumerate(pieces):

        @pl.when(me == k)
        def _(piece=piece):
            first[...] = piece[...]

        @pl.when(me == groups - 1 - k)
        def _(piece=piece):
            last[...] = piece[...]


def spread_out(source, near, field, along_x, along_y, down_y):
    _, channels, rows = source.shape
    part = channels // 4
    pairs = 2 * part
    upper = lax.broadcasted_iota(jnp.int32, (1, pairs, rows), 1) < part
    inside = lax.broadcasted_iota(jnp.int32, (1, pairs, rows), 2) < rows - 1
    field[near] = source[:, :pairs]
    coefs = source[:, pairs:]
    swapped = pltpu.roll(coefs, part, 1)
    along_x[near] = jnp.where(upper, coefs, swapped)
    flow_y = jnp.where(inside, jnp.where(upper, swapped, coefs), 0.0)
    along_y[near] = flow_y
    down_y[near] = pltpu.roll(flow_y, 1, 2)


def advance(parts):
    joined, fluxes, ends = [], [], []
    for field, along_x, along_y, down_y, first, last, before, behind in parts:
        near = pl.ds(first, last - first)
        here = field[near]
        inner = along_x[pl.ds(first, last - first - 1)] * (here[1:] - here[:-1])
        if before is None:
            before = along_x[first - 1] * (here[0] - field[first - 1])
        if behind is None:
            behind = along_x[last - 1] * (field[last] - here[-1])
        fluxes.append((before, behind))
        entering = jnp.concatenate([before[None], inner], 0)
        leaving = jnp.concatenate([inner, behind[None]], 0)
        joined.append((here, leaving, entering, along_y[near], down_y[near]))
        ends.append(sum(ends[-1:]) + last - first)
    here, leaving, entering, up, down = (jnp.concatenate(each, 0) for each in zip(*joined))
    rows = here.shape[-1]
    flux_y = up * (pltpu.roll(here, rows - 1, 2) - here)
    under = down * (here - pltpu.roll(here, 1, 2))
    result = here + leaving - entering + flux_y - under
    for (field, _, _, _, first, last, _, _), end in zip(parts, ends):
        field[pl.ds(first, last - first)] = result[end - last + first : end]
    return fluxes


def turn(columns, result, at):
    block = jnp.swapaxes(columns, 0, 1)
    for half in range(result.shape[0]):
        result[half, :, at] = block[:, :, half * LANES : (half + 1) * LANES]


def pack(result, turned, band_rows, bands, copies):
    halves, channels, count, _ = result.shape
    part = channels // 2
    total = bands.shape[0]
    for half in range(halves):
        for i in range(channels):
            turned[half, i] = pltpu.roll(result[half, i], i % part * CAP, 1)
    lane = lax.broadcasted_iota(jnp.int32, (count, LANES), 1)
    start = jnp.int32(0)
    for b in range(total):
        half = start // LANES
        offset = start - half * LANES
        beyond = lax.rem(half + 1, halves)
        place = jnp.bitwise_and(lane + (LANES - offset), LANES - 1)
        over = jnp.bitwise_and(place, CAP - 1) >= LANES - offset
        for v in range(2):
            here, there = turned[half, v * part], turned[beyond, v * part]
            for l in range(1, part):
                chosen = place >= l * CAP
                here = jnp.where(chosen, turned[half, v * part + l], here)
                there = jnp.where(chosen, turned[beyond, v * part + l], there)
            together = jnp.where(over, there, here)
            bands[b, v] = pltpu.roll(together, lax.rem(LANES - offset, LANES), 1)
        start = start + band_rows[b]
        if copies and (b + 1) * len(copies) % total == 0:
            copies[(b + 1) * len(copies) // total - 1].start()


def inner_kernel(groups, band_rows, *refs):
    pieces, field, along_x, along_y, down_y = refs[:groups], *refs[groups : groups + 4]
    sides, result, bands, ready, turned, sems = refs[groups + 4 :]
    width = pieces[0].shape[0]
    me = member(groups)
    for k, piece in enumerate(pieces):
        near = pl.ds(jnp.bitwise_xor(me, k) * width, width)
        spread_out(piece, near, field, along_x, along_y, down_y)
    span = groups * width
    for step in range(STEPS):
        last = step + 1
        behind = None
        for first in range(step + 1, span - 1 - step, BLOCK):
            last = min(first + BLOCK, span - 1 - step)
            piece = (field, along_x, along_y, down_y, first, last, behind, None)
            before, behind = advance([piece])[0]
            if first == step + 1:
                sides[0, step] = before
        sides[1, step] = behind
    for s in range(1, groups - 1):
        turn(field[pl.ds(s * width, width)], result, pl.ds((s - 1) * width, width))
    copy = pltpu.make_async_copy(ready, bands.at[:, :, pl.ds(0, span - 2 * width)], sems.at[0])
    pack(result, turned, band_rows, ready, [copy])
    copy.wait()


def end_kernel(groups, side, rows_far, halo, *refs):
    inner, sides, refs = refs[:4], refs[4], refs[5:]
    if side:
        other, _, bands, result, *end, ready, turned, band_rows, sems = refs
    else:
        ready, result, *end, turned, band_rows, sems = refs
    rows_copy = pltpu.make_async_copy(rows_far, band_rows, sems.at[groups])
    rows_copy.start()
    width = halo.shape[0]
    span = groups * width
    copies = []
    if side:
        other_copy = pltpu.make_async_copy(
            other, bands.at[:, :, pl.ds(span - 2 * width, width)], sems.at[groups + 1]
        )
        other_copy.start()
        each = bands.shape[0] // groups
        for i in range(groups):
            near = pl.ds(i * each, each)
            target = bands.at[near, :, pl.ds(span - width, width)]
            copies.append(pltpu.make_async_copy(ready.at[near], target, sems.at[i]))
    spread_out(halo, pl.ds(side * width, width), *end)
    for here, array in zip(end, inner):
        here[pl.ds((1 - side) * width, width)] = array[pl.ds(side * (span - width), width)]
    for step in range(STEPS):
        first = width - 1 - step if side else step + 1
        faces = (sides[1, step], None) if side else (None, sides[0, step])
        advance([(*end, first, first + width, *faces)])
    turn(end[0][pl.ds((1 - side) * width, width)], result, pl.ds(0, width))
    rows_copy.wait()
    pack(result, turned, band_rows, ready, copies)
    if side:
        for copy in copies + [other_copy]:
            copy.wait()


def strips_kernel(groups, low, inner, high, *refs):
    strips, whole = refs[:groups], refs[groups]
    halves, _, width, _ = low.shape
    span = groups * width
    me = member(groups)
    whole[:, :, pl.ds(0, width)] = low[...]
    whole[:, :, pl.ds(width, span - 2 * width)] = inner[...]
    whole[:, :, pl.ds(span - width, width)] = high[...]
    for k in range(groups):
        s = jnp.bitwise_xor(me, k)
        for half in range(halves):
            strips[k][:, :, half * LANES : (half + 1) * LANES] = whole[
                half, :, pl.ds(pl.multiple_of(s * width, width), width)
            ]


def filtered(taps, v, l, levels, whole):
    total = whole[v, l]
    for tap in range(TAPS):
        other = l + tap - TAPS // 2
        if 0 <= other < levels:
            total = total + taps(tap, v, l) * whole[v, other]
    return total


def increment_kernel(groups, band_rows, weights, *refs):
    pieces, out, taps, keep, whole = refs[:groups], *refs[groups:]
    variables, levels = out.shape[:2]
    part = levels // groups
    me = member(groups)
    for k in range(groups):
        near = pl.ds(jnp.bitwise_xor(me, k) * part, part)
        for v in range(variables):
            whole[v, near] = pieces[k][pl.ds(v * part, part)]
    for v in range(variables):
        for l in range(levels):
            out[v, l] = filtered(lambda a, b, c: weights[a, b, c], v, l, levels, whole)
            for tap in range(TAPS):
                taps[tap, v, l] = jnp.full(taps.shape[3:], weights[tap, v, l])
    row = lax.broadcasted_iota(jnp.int32, keep.shape, 0)
    keep[...] = (row < band_rows[lax.axis_index("band")]).astype(jnp.int32)


def band_kernel(groups, width, taps, keep, arrived, out, whole, ready, sems):
    variables, levels, height, _ = out.shape
    part = levels // groups
    count, _, span, _ = arrived.shape
    inside = span - 2 * width
    mine = keep[...] > 0
    copies = []
    for v in range(variables):
        for q in range(groups):
            blocks = []
            for s in range(q, count, groups):
                blocks += [arrived[s, v, inside : inside + width], arrived[s, v, :inside]]
                blocks += [arrived[s, v, inside + width :]]
            flat = jnp.transpose(jnp.concatenate(blocks, 0))
            for l in range(part):
                whole[v, q * part + l] = flat[l * height : (l + 1) * height]
    for v in range(variables):
        for l in range(levels):
            total = filtered(lambda a, b, c: taps[a, b, c], v, l, levels, whole)
            ready[v, l] = jnp.where(mine, total, 0.0)
            if (l + 1) % part == 0:
                near = pl.ds(l + 1 - part, part)
                i = len(copies)
                copies.append(
                    pltpu.make_async_copy(ready.at[v, near], out.at[v, near], sems.at[i])
                )
                copies[i].start()
    for copy in copies:
        copy.wait()


def shards(mesh_shape, background, scale_x, scale_y, filter_bands, band_rows):
    variables, levels, width, rows = background.shape
    count, blocks = mesh_shape["band"], mesh_shape["lon"]
    groups = math.isqrt(count)
    part = levels // groups
    channels = (variables + 2) * part
    f32 = jnp.float32

    def struct(*shape):
        return jax.ShapeDtypeStruct(shape, f32)

    piece = struct(width, channels, rows)
    parted = pl.pallas_call(
        regroup_kernel,
        out_shape=[piece] * groups,
        in_specs=[HBM] * 3,
        out_specs=[VMEM] * groups,
        scratch_shapes=[pltpu.VMEM(a.shape, f32) for a in (background, scale_x, scale_y)]
        + [pltpu.SemaphoreType.DMA((groups, 3))],
        compiler_params=ROOM,
        name="regroup",
    )(*(pltpu.with_memory_space_constraint(a, pltpu.HBM) for a in (background, scale_x, scale_y)))
    weights = jnp.transpose(filter_bands, (1, 0, 2))

    def exchanged(pieces):
        return [pieces[0]] + [
            lax.ppermute(pieces[k], "band", [(i, i ^ k) for i in range(count)])
            for k in range(1, groups)
        ]

    mine = exchanged(parted)
    first, last = pl.pallas_call(
        edges_kernel,
        out_shape=[piece] * 2,
        in_specs=[VMEM] * groups,
        out_specs=[VMEM] * 2,
        compiler_params=ROOM,
        name="edges",
    )(*mine)

    def shifted(by):
        total = count * blocks
        pairs = []
        for source in range(total):
            target = (source + by) % total
            pairs.append(
                (
                    source % count * blocks + source // count,
                    target % count * blocks + target // count,
                )
            )
        return pairs

    axes = ("band", "lon")
    low = lax.ppermute(last, axes, shifted(groups))
    high = lax.ppermute(first, axes, shifted(-groups))
    span = groups * width
    inside = span - 2 * width
    halves = rows // LANES
    both = variables * part
    inner = pl.pallas_call(
        functools.partial(inner_kernel, groups),
        out_shape=[struct(span, both, rows)] * 4
        + [
            struct(2, STEPS, both, rows),
            struct(halves, both, inside, LANES),
            struct(count, variables, span, LANES),
        ],
        in_specs=[SMEM] + [VMEM] * groups,
        out_specs=[VMEM] * 6 + [HBM],
        scratch_shapes=[
            pltpu.VMEM((count, variables, inside, LANES), f32),
            pltpu.VMEM((halves, both, inside, LANES), f32),
            pltpu.SemaphoreType.DMA((1,)),
        ],
        compiler_params=ROOM,
        cost_estimate=pl.CostEstimate(
            flops=20 * STEPS * span * both * rows, bytes_accessed=2**20, transcendentals=0
        ),
        name="inner",
    )(band_rows, *mine)
    *arrays, inner_result, bands = inner

    cut = struct(count, variables, width, LANES)
    turned = struct(halves, both, width, LANES)
    scratch = [pltpu.VMEM((2 * width, both, rows), f32)] * 4
    small = [
        pltpu.VMEM(turned.shape, f32),
        pltpu.SMEM(band_rows.shape, band_rows.dtype),
        pltpu.SemaphoreType.DMA((groups + 2,)),
    ]
    low_bands, low_result = pl.pallas_call(
        functools.partial(end_kernel, groups, 0),
        out_shape=[cut, turned],
        in_specs=[HBM] + [VMEM] * 6,
        out_specs=[VMEM] * 2,
        scratch_shapes=scratch + small,
        compiler_params=ROOM,
        name="low_end",
    )(band_rows, low, *arrays)
    bands, high_result = pl.pallas_call(
        functools.partial(end_kernel, groups, 1),
        out_shape=[struct(count, variables, span, LANES), turned],
        in_specs=[HBM] + [VMEM] * 7 + [HBM],
        out_specs=[HBM, VMEM],
        input_output_aliases={8: 0},
        scratch_shapes=scratch + [pltpu.VMEM(cut.shape, f32)] + small,
        compiler_params=ROOM,
        name="high_end",
    )(band_rows, high, *arrays, low_bands, bands)
    strips = pl.pallas_call(
        functools.partial(strips_kernel, groups),
        out_shape=[struct(both, width, rows)] * groups,
        in_specs=[VMEM] * 3,
        out_specs=[VMEM] * groups,
        scratch_shapes=[pltpu.VMEM((halves, both, span, LANES), f32)],
        compiler_params=ROOM,
        name="strips",
    )(low_result, inner_result, high_result)
    arrived = lax.all_to_all(bands, "band", split_axis=0, concat_axis=0, tiled=True)
    pieces = exchanged(strips)
    increment, taps, keep = pl.pallas_call(
        functools.partial(increment_kernel, groups),
        out_shape=[
            struct(*background.shape),
            struct(TAPS, variables, levels, 1, count * width),
            jax.ShapeDtypeStruct((CAP, count * width), jnp.int32),
        ],
        in_specs=[SMEM, SMEM] + [VMEM] * groups,
        out_specs=[VMEM] * 3,
        scratch_shapes=[pltpu.VMEM((variables, levels, width, rows), f32)],
        compiler_params=ROOM,
        name="increment",
    )(band_rows, weights, *pieces)
    band_field = pl.pallas_call(
        functools.partial(band_kernel, groups, width),
        out_shape=struct(variables, levels, CAP, count * width),
        in_specs=[VMEM] * 3,
        out_specs=HBM,
        scratch_shapes=[pltpu.VMEM((variables, levels, CAP, count * width), f32)] * 2
        + [pltpu.SemaphoreType.DMA((variables * groups,))],
        compiler_params=ROOM,
        name="bands",
    )(taps, keep, arrived)
    return increment, band_field


def solution(mesh):
    in_specs = (
        P(None, None, ("lon", "band"), None),
        P(None, ("lon", "band"), None),
        P(None, ("lon", "band"), None),
        P(),
        P(),
    )
    out_specs = (P(None, None, ("lon", "band"), None), P(None, None, "band", "lon"))
    return jax.shard_map(
        functools.partial(shards, dict(mesh.shape)),
        mesh=mesh,
        in_specs=in_specs,
        out_specs=out_specs,
        check_vma=False,
    )
```

```python
import functools
import math

import jax
import jax.numpy as jnp
from jax import lax
from jax.experimental import pallas as pl
from jax.experimental.pallas import tpu as pltpu
from jax.sharding import PartitionSpec as P

STEPS = 8
CAP = 32
LANES = 128
TAPS = 5
BLOCK = 16
VMEM = pl.BlockSpec(memory_space=pltpu.VMEM)
SMEM = pl.BlockSpec(memory_space=pltpu.SMEM)
HBM = pl.BlockSpec(memory_space=pltpu.HBM)
ROOM = pltpu.CompilerParams(vmem_limit_bytes=8 * 2**20)


def member(groups):
    return lax.rem(lax.axis_index("band"), groups)


def regroup_kernel(background, scale_x, scale_y, *refs):
    *pieces, field, along_x, along_y, sems = refs
    variables, levels = background.shape[:2]
    part = levels // len(pieces)
    me = member(len(pieces))
    parts, copies = [], []
    for k in range(len(pieces)):
        near = pl.ds(jnp.bitwise_xor(me, k) * part, part)
        parts.append(near)
        copies.append(
            [
                pltpu.make_async_copy(background.at[:, near], field.at[:, near], sems.at[k, 0]),
                pltpu.make_async_copy(scale_x.at[near], along_x.at[near], sems.at[k, 1]),
                pltpu.make_async_copy(scale_y.at[near], along_y.at[near], sems.at[k, 2]),
            ]
        )
        for copy in copies[k]:
            copy.start()
    for near, piece, each in zip(parts, pieces, copies):
        for copy in each:
            copy.wait()
        sources = [field[v, near] for v in range(variables)]
        sources += [along_x[near], along_y[near]]
        piece[...] = jnp.swapaxes(jnp.concatenate(sources, 0), 0, 1)


def edges_kernel(*refs):
    *pieces, first, last = refs
    groups = len(pieces)
    me = member(groups)
    for k, piece in enumerate(pieces):

        @pl.when(me == k)
        def _(piece=piece):
            first[...] = piece[...]

        @pl.when(me == groups - 1 - k)
        def _(piece=piece):
            last[...] = piece[...]


def spread_out(source, near, field, along_x, along_y, down_y):
    _, channels, rows = source.shape
    part = channels // 4
    pairs = 2 * part
    upper = lax.broadcasted_iota(jnp.int32, (1, pairs, rows), 1) < part
    inside = lax.broadcasted_iota(jnp.int32, (1, pairs, rows), 2) < rows - 1
    field[near] = source[:, :pairs]
    coefs = source[:, pairs:]
    swapped = pltpu.roll(coefs, part, 1)
    along_x[near] = jnp.where(upper, coefs, swapped)
    flow_y = jnp.where(inside, jnp.where(upper, swapped, coefs), 0.0)
    along_y[near] = flow_y
    down_y[near] = pltpu.roll(flow_y, 1, 2)


def advance(parts):
    joined, fluxes, ends = [], [], []
    for field, along_x, along_y, down_y, first, last, before, behind in parts:
        near = pl.ds(first, last - first)
        here = field[near]
        inner = along_x[pl.ds(first, last - first - 1)] * (here[1:] - here[:-1])
        if before is None:
            before = along_x[first - 1] * (here[0] - field[first - 1])
        if behind is None:
            behind = along_x[last - 1] * (field[last] - here[-1])
        fluxes.append((before, behind))
        entering = jnp.concatenate([before[None], inner], 0)
        leaving = jnp.concatenate([inner, behind[None]], 0)
        joined.append((here, leaving, entering, along_y[near], down_y[near]))
        ends.append(sum(ends[-1:]) + last - first)
    here, leaving, entering, up, down = (jnp.concatenate(each, 0) for each in zip(*joined))
    rows = here.shape[-1]
    flux_y = up * (pltpu.roll(here, rows - 1, 2) - here)
    under = down * (here - pltpu.roll(here, 1, 2))
    result = here + leaving - entering + flux_y - under
    for (field, _, _, _, first, last, _, _), end in zip(parts, ends):
        field[pl.ds(first, last - first)] = result[end - last + first : end]
    return fluxes


def turn(columns, result, at):
    block = jnp.swapaxes(columns, 0, 1)
    for half in range(result.shape[0]):
        result[half, :, at] = block[:, :, half * LANES : (half + 1) * LANES]


def pack(result, turned, band_rows, bands, copies):
    halves, channels, count, _ = result.shape
    part = channels // 2
    total = bands.shape[0]
    for half in range(halves):
        for i in range(channels):
            turned[half, i] = pltpu.roll(result[half, i], i % part * CAP, 1)
    lane = lax.broadcasted_iota(jnp.int32, (count, LANES), 1)
    start = jnp.int32(0)
    for b in range(total):
        half = start // LANES
        offset = start - half * LANES
        beyond = lax.rem(half + 1, halves)
        place = jnp.bitwise_and(lane + (LANES - offset), LANES - 1)
        over = jnp.bitwise_and(place, CAP - 1) >= LANES - offset
        for v in range(2):
            here, there = turned[half, v * part], turned[beyond, v * part]
            for l in range(1, part):
                chosen = place >= l * CAP
                here = jnp.where(chosen, turned[half, v * part + l], here)
                there = jnp.where(chosen, turned[beyond, v * part + l], there)
            together = jnp.where(over, there, here)
            bands[b, v] = pltpu.roll(together, lax.rem(LANES - offset, LANES), 1)
        start = start + band_rows[b]
        if (b + 1) * len(copies) % total == 0:
            copies[(b + 1) * len(copies) // total - 1].start()


def inner_kernel(groups, band_rows, *refs):
    pieces, field, along_x, along_y, down_y = refs[:groups], *refs[groups : groups + 4]
    sides, result, bands, ready, turned, sems = refs[groups + 4 :]
    width = pieces[0].shape[0]
    me = member(groups)
    for k, piece in enumerate(pieces):
        near = pl.ds(jnp.bitwise_xor(me, k) * width, width)
        spread_out(piece, near, field, along_x, along_y, down_y)
    span = groups * width
    for step in range(STEPS):
        last = step + 1
        behind = None
        for first in range(step + 1, span - 1 - step, BLOCK):
            last = min(first + BLOCK, span - 1 - step)
            piece = (field, along_x, along_y, down_y, first, last, behind, None)
            before, behind = advance([piece])[0]
            if first == step + 1:
                sides[0, step] = before
        sides[1, step] = behind
    for s in range(1, groups - 1):
        turn(field[pl.ds(s * width, width)], result, pl.ds((s - 1) * width, width))
    copy = pltpu.make_async_copy(ready, bands.at[:, :, pl.ds(0, span - 2 * width)], sems.at[0])
    pack(result, turned, band_rows, ready, [copy])
    copy.wait()


def end_kernel(groups, side, rows_far, halo, *refs):
    inner, sides, _, bands, result = refs[:4], *refs[4:8]
    end, ready, turned, band_rows, sems = refs[8:12], *refs[12:]
    rows_copy = pltpu.make_async_copy(rows_far, band_rows, sems.at[groups])
    rows_copy.start()
    width = halo.shape[0]
    span = groups * width
    spread_out(halo, pl.ds(side * width, width), *end)
    for here, array in zip(end, inner):
        here[pl.ds((1 - side) * width, width)] = array[pl.ds(side * (span - width), width)]
    for step in range(STEPS):
        first = width - 1 - step if side else step + 1
        faces = (sides[1, step], None) if side else (None, sides[0, step])
        advance([(*end, first, first + width, *faces)])
    turn(end[0][pl.ds((1 - side) * width, width)], result, pl.ds(0, width))

    copies = []
    each = bands.shape[0] // groups
    for i in range(groups):
        near = pl.ds(i * each, each)
        target = bands.at[near, :, pl.ds(span - (2 - side) * width, width)]
        copies.append(pltpu.make_async_copy(ready.at[near], target, sems.at[i]))
    rows_copy.wait()
    pack(result, turned, band_rows, ready, copies)
    for copy in copies:
        copy.wait()


def strips_kernel(groups, low, inner, high, *refs):
    strips, whole = refs[:groups], refs[groups]
    halves, _, width, _ = low.shape
    span = groups * width
    me = member(groups)
    whole[:, :, pl.ds(0, width)] = low[...]
    whole[:, :, pl.ds(width, span - 2 * width)] = inner[...]
    whole[:, :, pl.ds(span - width, width)] = high[...]
    for k in range(groups):
        s = jnp.bitwise_xor(me, k)
        for half in range(halves):
            strips[k][:, :, half * LANES : (half + 1) * LANES] = whole[
                half, :, pl.ds(pl.multiple_of(s * width, width), width)
            ]


def filtered(taps, v, l, levels, whole):
    total = whole[v, l]
    for tap in range(TAPS):
        other = l + tap - TAPS // 2
        if 0 <= other < levels:
            total = total + taps(tap, v, l) * whole[v, other]
    return total


def increment_kernel(groups, band_rows, weights, *refs):
    pieces, out, taps, keep, whole = refs[:groups], *refs[groups:]
    variables, levels = out.shape[:2]
    part = levels // groups
    me = member(groups)
    for k in range(groups):
        near = pl.ds(jnp.bitwise_xor(me, k) * part, part)
        for v in range(variables):
            whole[v, near] = pieces[k][pl.ds(v * part, part)]
    for v in range(variables):
        for l in range(levels):
            out[v, l] = filtered(lambda a, b, c: weights[a, b, c], v, l, levels, whole)
            for tap in range(TAPS):
                taps[tap, v, l] = jnp.full(taps.shape[3:], weights[tap, v, l])
    row = lax.broadcasted_iota(jnp.int32, keep.shape, 0)
    keep[...] = (row < band_rows[lax.axis_index("band")]).astype(jnp.int32)


def band_kernel(groups, width, taps, keep, arrived, out, whole, ready, sems):
    variables, levels, height, _ = out.shape
    part = levels // groups
    count, _, span, _ = arrived.shape
    inside = span - 2 * width
    mine = keep[...] > 0
    copies = []
    for v in range(variables):
        for q in range(groups):
            blocks = []
            for s in range(q, count, groups):
                blocks += [arrived[s, v, inside : inside + width], arrived[s, v, :inside]]
                blocks += [arrived[s, v, inside + width :]]
            flat = jnp.transpose(jnp.concatenate(blocks, 0))
            for l in range(part):
                whole[v, q * part + l] = flat[l * height : (l + 1) * height]
    for v in range(variables):
        for l in range(levels):
            total = filtered(lambda a, b, c: taps[a, b, c], v, l, levels, whole)
            ready[v, l] = jnp.where(mine, total, 0.0)
            if (l + 1) % part == 0:
                near = pl.ds(l + 1 - part, part)
                i = len(copies)
                copies.append(
                    pltpu.make_async_copy(ready.at[v, near], out.at[v, near], sems.at[i])
                )
                copies[i].start()
    for copy in copies:
        copy.wait()


def shards(mesh_shape, background, scale_x, scale_y, filter_bands, band_rows):
    variables, levels, width, rows = background.shape
    count, blocks = mesh_shape["band"], mesh_shape["lon"]
    groups = math.isqrt(count)
    part = levels // groups
    channels = (variables + 2) * part
    f32 = jnp.float32

    def struct(*shape):
        return jax.ShapeDtypeStruct(shape, f32)

    piece = struct(width, channels, rows)
    parted = pl.pallas_call(
        regroup_kernel,
        out_shape=[piece] * groups,
        in_specs=[HBM] * 3,
        out_specs=[VMEM] * groups,
        scratch_shapes=[pltpu.VMEM(a.shape, f32) for a in (background, scale_x, scale_y)]
        + [pltpu.SemaphoreType.DMA((groups, 3))],
        compiler_params=ROOM,
        name="regroup",
    )(*(pltpu.with_memory_space_constraint(a, pltpu.HBM) for a in (background, scale_x, scale_y)))
    weights = jnp.transpose(filter_bands, (1, 0, 2))

    def exchanged(pieces):
        return [pieces[0]] + [
            lax.ppermute(pieces[k], "band", [(i, i ^ k) for i in range(count)])
            for k in range(1, groups)
        ]

    mine = exchanged(parted)
    first, last = pl.pallas_call(
        edges_kernel,
        out_shape=[piece] * 2,
        in_specs=[VMEM] * groups,
        out_specs=[VMEM] * 2,
        compiler_params=ROOM,
        name="edges",
    )(*mine)

    def shifted(by):
        total = count * blocks
        pairs = []
        for source in range(total):
            target = (source + by) % total
            pairs.append(
                (
                    source % count * blocks + source // count,
                    target % count * blocks + target // count,
                )
            )
        return pairs

    axes = ("band", "lon")
    low = lax.ppermute(last, axes, shifted(groups))
    high = lax.ppermute(first, axes, shifted(-groups))
    span = groups * width
    inside = span - 2 * width
    halves = rows // LANES
    both = variables * part
    inner = pl.pallas_call(
        functools.partial(inner_kernel, groups),
        out_shape=[struct(span, both, rows)] * 4
        + [
            struct(2, STEPS, both, rows),
            struct(halves, both, inside, LANES),
            struct(count, variables, span, LANES),
        ],
        in_specs=[SMEM] + [VMEM] * groups,
        out_specs=[VMEM] * 6 + [HBM],
        scratch_shapes=[
            pltpu.VMEM((count, variables, inside, LANES), f32),
            pltpu.VMEM((halves, both, inside, LANES), f32),
            pltpu.SemaphoreType.DMA((1,)),
        ],
        compiler_params=ROOM,
        cost_estimate=pl.CostEstimate(
            flops=20 * STEPS * span * both * rows, bytes_accessed=2**20, transcendentals=0
        ),
        name="inner",
    )(band_rows, *mine)
    *arrays, inner_result, bands = inner

    def finished(side, halo, bands):
        return pl.pallas_call(
            functools.partial(end_kernel, groups, side),
            out_shape=[
                struct(count, variables, span, LANES),
                struct(halves, both, width, LANES),
            ],
            in_specs=[HBM] + [VMEM] * 6 + [HBM],
            out_specs=[HBM, VMEM],
            input_output_aliases={7: 0},
            scratch_shapes=[pltpu.VMEM((2 * width, both, rows), f32)] * 4
            + [
                pltpu.VMEM((count, variables, width, LANES), f32),
                pltpu.VMEM((halves, both, width, LANES), f32),
                pltpu.SMEM(band_rows.shape, band_rows.dtype),
                pltpu.SemaphoreType.DMA((groups + 1,)),
            ],
            compiler_params=ROOM,
            name="high_end" if side else "low_end",
        )(band_rows, halo, *arrays, bands)

    bands, low_result = finished(0, low, bands)
    bands, high_result = finished(1, high, bands)
    strips = pl.pallas_call(
        functools.partial(strips_kernel, groups),
        out_shape=[struct(both, width, rows)] * groups,
        in_specs=[VMEM] * 3,
        out_specs=[VMEM] * groups,
        scratch_shapes=[pltpu.VMEM((halves, both, span, LANES), f32)],
        compiler_params=ROOM,
        name="strips",
    )(low_result, inner_result, high_result)
    arrived = lax.all_to_all(bands, "band", split_axis=0, concat_axis=0, tiled=True)
    pieces = exchanged(strips)
    increment, taps, keep = pl.pallas_call(
        functools.partial(increment_kernel, groups),
        out_shape=[
            struct(*background.shape),
            struct(TAPS, variables, levels, 1, count * width),
            jax.ShapeDtypeStruct((CAP, count * width), jnp.int32),
        ],
        in_specs=[SMEM, SMEM] + [VMEM] * groups,
        out_specs=[VMEM] * 3,
        scratch_shapes=[pltpu.VMEM((variables, levels, width, rows), f32)],
        compiler_params=ROOM,
        name="increment",
    )(band_rows, weights, *pieces)
    band_field = pl.pallas_call(
        functools.partial(band_kernel, groups, width),
        out_shape=struct(variables, levels, CAP, count * width),
        in_specs=[VMEM] * 3,
        out_specs=HBM,
        scratch_shapes=[pltpu.VMEM((variables, levels, CAP, count * width), f32)] * 2
        + [pltpu.SemaphoreType.DMA((variables * groups,))],
        compiler_params=ROOM,
        name="bands",
    )(taps, keep, arrived)
    return increment, band_field


def solution(mesh):
    in_specs = (
        P(None, None, ("lon", "band"), None),
        P(None, ("lon", "band"), None),
        P(None, ("lon", "band"), None),
        P(),
        P(),
    )
    out_specs = (P(None, None, ("lon", "band"), None), P(None, None, "band", "lon"))
    return jax.shard_map(
        functools.partial(shards, dict(mesh.shape)),
        mesh=mesh,
        in_specs=in_specs,
        out_specs=out_specs,
        check_vma=False,
    )
```

```python
import functools
import math

import jax
import jax.numpy as jnp
from jax import lax
from jax.experimental import pallas as pl
from jax.experimental.pallas import tpu as pltpu
from jax.sharding import PartitionSpec as P

STEPS = 8
CAP = 32
LANES = 128
TAPS = 5
BLOCK = 16
VMEM = pl.BlockSpec(memory_space=pltpu.VMEM)
SMEM = pl.BlockSpec(memory_space=pltpu.SMEM)
HBM = pl.BlockSpec(memory_space=pltpu.HBM)
ROOM = pltpu.CompilerParams(vmem_limit_bytes=8 * 2**20)


def member(groups):
    return lax.rem(lax.axis_index("band"), groups)


def regroup_kernel(background, scale_x, scale_y, *refs):
    *pieces, sems = refs
    variables, levels = background.shape[:2]
    part = levels // len(pieces)
    me = member(len(pieces))
    copies = []
    for k, piece in enumerate(pieces):
        near = pl.ds(jnp.bitwise_xor(me, k) * part, part)
        sources = [background.at[v, near] for v in range(variables)]
        sources += [scale_x.at[near], scale_y.at[near]]
        for i, source in enumerate(sources):
            target = piece.at[pl.ds(i * part, part)]
            copies.append(pltpu.make_async_copy(source, target, sems.at[k, i]))
    for copy in copies:
        copy.start()
    for copy in copies:
        copy.wait()


def edges_kernel(*refs):
    *pieces, first, last = refs
    groups = len(pieces)
    me = member(groups)
    for k, piece in enumerate(pieces):

        @pl.when(me == k)
        def _(piece=piece):
            first[...] = piece[...]

        @pl.when(me == groups - 1 - k)
        def _(piece=piece):
            last[...] = piece[...]


def spread_out(source, near, field, along_x, along_y, down_y):
    channels, _, rows = source.shape
    part = channels // 4
    pairs = 2 * part
    upper = lax.broadcasted_iota(jnp.int32, (1, pairs, rows), 1) < part
    inside = lax.broadcasted_iota(jnp.int32, (1, pairs, rows), 2) < rows - 1
    flow = jnp.swapaxes(source[...], 0, 1)
    field[near] = flow[:, :pairs]
    coefs = flow[:, pairs:]
    swapped = pltpu.roll(coefs, part, 1)
    along_x[near] = jnp.where(upper, coefs, swapped)
    flow_y = jnp.where(inside, jnp.where(upper, swapped, coefs), 0.0)
    along_y[near] = flow_y
    down_y[near] = pltpu.roll(flow_y, 1, 2)


def advance(parts):
    joined, fluxes, ends = [], [], []
    for field, along_x, along_y, down_y, first, last, before, behind in parts:
        near = pl.ds(first, last - first)
        here = field[near]
        inner = along_x[pl.ds(first, last - first - 1)] * (here[1:] - here[:-1])
        if before is None:
            before = along_x[first - 1] * (here[0] - field[first - 1])
        if behind is None:
            behind = along_x[last - 1] * (field[last] - here[-1])
        fluxes.append((before, behind))
        entering = jnp.concatenate([before[None], inner], 0)
        leaving = jnp.concatenate([inner, behind[None]], 0)
        joined.append((here, leaving, entering, along_y[near], down_y[near]))
        ends.append(sum(ends[-1:]) + last - first)
    here, leaving, entering, up, down = (jnp.concatenate(each, 0) for each in zip(*joined))
    rows = here.shape[-1]
    flux_y = up * (pltpu.roll(here, rows - 1, 2) - here)
    under = down * (here - pltpu.roll(here, 1, 2))
    result = here + leaving - entering + flux_y - under
    for (field, _, _, _, first, last, _, _), end in zip(parts, ends):
        field[pl.ds(first, last - first)] = result[end - last + first : end]
    return fluxes


def turn(columns, result, at):
    block = jnp.swapaxes(columns, 0, 1)
    for half in range(result.shape[0]):
        result[half, :, at] = block[:, :, half * LANES : (half + 1) * LANES]


def pack(result, band_rows, bands, copies):
    halves, channels, count, _ = result.shape
    part = channels // 2
    total = bands.shape[0]
    lane = lax.broadcasted_iota(jnp.int32, (count, LANES), 1)
    start = jnp.int32(0)
    for b in range(total):
        half = start // LANES
        offset = start - half * LANES
        beyond = lax.rem(half + 1, halves)
        for v in range(2):
            packed = None
            for l in range(part):
                i = v * part + l
                window = jnp.where(lane >= offset, result[half, i], result[beyond, i])
                shift = lax.rem(LANES + l * CAP - offset, LANES)
                turned = pltpu.roll(window, shift, 1)
                packed = turned if l == 0 else jnp.where(lane >= l * CAP, turned, packed)
            bands[b, v] = packed
        start = start + band_rows[b]
        if (b + 1) * len(copies) % total == 0:
            copies[(b + 1) * len(copies) // total - 1].start()


def inner_kernel(groups, band_rows, *refs):
    pieces, field, along_x, along_y, down_y = refs[:groups], *refs[groups : groups + 4]
    sides, result, bands, ready, sems = refs[groups + 4 :]
    width = pieces[0].shape[1]
    me = member(groups)
    for k, piece in enumerate(pieces):
        near = pl.ds(jnp.bitwise_xor(me, k) * width, width)
        spread_out(piece, near, field, along_x, along_y, down_y)
    span = groups * width
    for step in range(STEPS):
        last = step + 1
        behind = None
        for first in range(step + 1, span - 1 - step, BLOCK):
            last = min(first + BLOCK, span - 1 - step)
            piece = (field, along_x, along_y, down_y, first, last, behind, None)
            before, behind = advance([piece])[0]
            if first == step + 1:
                sides[0, step] = before
        sides[1, step] = behind
    for s in range(1, groups - 1):
        turn(field[pl.ds(s * width, width)], result, pl.ds((s - 1) * width, width))
    copy = pltpu.make_async_copy(ready, bands.at[:, :, pl.ds(0, span - 2 * width)], sems.at[0])
    pack(result, band_rows, ready, [copy])
    copy.wait()


def end_kernel(groups, side, rows_far, halo, *refs):
    inner, sides, _, bands, result = refs[:4], *refs[4:8]
    end, ready, band_rows, sems = refs[8:12], *refs[12:]
    rows_copy = pltpu.make_async_copy(rows_far, band_rows, sems.at[groups])
    rows_copy.start()
    width = halo.shape[1]
    span = groups * width
    spread_out(halo, pl.ds(side * width, width), *end)
    for here, array in zip(end, inner):
        here[pl.ds((1 - side) * width, width)] = array[pl.ds(side * (span - width), width)]
    for step in range(STEPS):
        first = width - 1 - step if side else step + 1
        faces = (sides[1, step], None) if side else (None, sides[0, step])
        advance([(*end, first, first + width, *faces)])
    turn(end[0][pl.ds((1 - side) * width, width)], result, pl.ds(0, width))

    copies = []
    each = bands.shape[0] // groups
    for i in range(groups):
        near = pl.ds(i * each, each)
        target = bands.at[near, :, pl.ds(span - (2 - side) * width, width)]
        copies.append(pltpu.make_async_copy(ready.at[near], target, sems.at[i]))
    rows_copy.wait()
    pack(result, band_rows, ready, copies)
    for copy in copies:
        copy.wait()


def strips_kernel(groups, low, inner, high, *refs):
    strips, whole = refs[:groups], refs[groups]
    halves, _, width, _ = low.shape
    span = groups * width
    me = member(groups)
    whole[:, :, pl.ds(0, width)] = low[...]
    whole[:, :, pl.ds(width, span - 2 * width)] = inner[...]
    whole[:, :, pl.ds(span - width, width)] = high[...]
    for k in range(groups):
        s = jnp.bitwise_xor(me, k)
        for half in range(halves):
            strips[k][:, :, half * LANES : (half + 1) * LANES] = whole[
                half, :, pl.ds(pl.multiple_of(s * width, width), width)
            ]


def filtered(taps, v, l, levels, whole):
    total = whole[v, l]
    for tap in range(TAPS):
        other = l + tap - TAPS // 2
        if 0 <= other < levels:
            total = total + taps(tap, v, l) * whole[v, other]
    return total


def increment_kernel(groups, band_rows, weights, *refs):
    pieces, out, taps, keep, whole = refs[:groups], *refs[groups:]
    variables, levels = out.shape[:2]
    part = levels // groups
    me = member(groups)
    for k in range(groups):
        near = pl.ds(jnp.bitwise_xor(me, k) * part, part)
        for v in range(variables):
            whole[v, near] = pieces[k][pl.ds(v * part, part)]
    for v in range(variables):
        for l in range(levels):
            out[v, l] = filtered(lambda a, b, c: weights[a, b, c], v, l, levels, whole)
            for tap in range(TAPS):
                taps[tap, v, l] = jnp.full(taps.shape[3:], weights[tap, v, l])
    row = lax.broadcasted_iota(jnp.int32, keep.shape, 0)
    keep[...] = (row < band_rows[lax.axis_index("band")]).astype(jnp.int32)


def band_kernel(groups, width, taps, keep, arrived, out, whole, ready, sems):
    variables, levels, height, _ = out.shape
    part = levels // groups
    count, _, span, _ = arrived.shape
    inside = span - 2 * width
    mine = keep[...] > 0
    copies = []
    for v in range(variables):
        for q in range(groups):
            blocks = []
            for s in range(q, count, groups):
                blocks += [arrived[s, v, inside : inside + width], arrived[s, v, :inside]]
                blocks += [arrived[s, v, inside + width :]]
            flat = jnp.transpose(jnp.concatenate(blocks, 0))
            for l in range(part):
                whole[v, q * part + l] = flat[l * height : (l + 1) * height]
    for v in range(variables):
        for l in range(levels):
            total = filtered(lambda a, b, c: taps[a, b, c], v, l, levels, whole)
            ready[v, l] = jnp.where(mine, total, 0.0)
            if (l + 1) % part == 0:
                near = pl.ds(l + 1 - part, part)
                i = len(copies)
                copies.append(
                    pltpu.make_async_copy(ready.at[v, near], out.at[v, near], sems.at[i])
                )
                copies[i].start()
    for copy in copies:
        copy.wait()


def shards(mesh_shape, background, scale_x, scale_y, filter_bands, band_rows):
    variables, levels, width, rows = background.shape
    count, blocks = mesh_shape["band"], mesh_shape["lon"]
    groups = math.isqrt(count)
    part = levels // groups
    channels = (variables + 2) * part
    f32 = jnp.float32

    def struct(*shape):
        return jax.ShapeDtypeStruct(shape, f32)

    piece = struct(channels, width, rows)
    parted = pl.pallas_call(
        regroup_kernel,
        out_shape=[piece] * groups,
        in_specs=[HBM] * 3,
        out_specs=[VMEM] * groups,
        scratch_shapes=[pltpu.SemaphoreType.DMA((groups, variables + 2))],
        compiler_params=ROOM,
        name="regroup",
    )(*(pltpu.with_memory_space_constraint(a, pltpu.HBM) for a in (background, scale_x, scale_y)))
    weights = jnp.transpose(filter_bands, (1, 0, 2))

    def exchanged(pieces):
        return [pieces[0]] + [
            lax.ppermute(pieces[k], "band", [(i, i ^ k) for i in range(count)])
            for k in range(1, groups)
        ]

    mine = exchanged(parted)
    first, last = pl.pallas_call(
        edges_kernel,
        out_shape=[piece] * 2,
        in_specs=[VMEM] * groups,
        out_specs=[VMEM] * 2,
        compiler_params=ROOM,
        name="edges",
    )(*mine)

    def shifted(by):
        total = count * blocks
        pairs = []
        for source in range(total):
            target = (source + by) % total
            pairs.append(
                (
                    source % count * blocks + source // count,
                    target % count * blocks + target // count,
                )
            )
        return pairs

    axes = ("band", "lon")
    low = lax.ppermute(last, axes, shifted(groups))
    high = lax.ppermute(first, axes, shifted(-groups))
    span = groups * width
    inside = span - 2 * width
    halves = rows // LANES
    both = variables * part
    inner = pl.pallas_call(
        functools.partial(inner_kernel, groups),
        out_shape=[struct(span, both, rows)] * 4
        + [
            struct(2, STEPS, both, rows),
            struct(halves, both, inside, LANES),
            struct(count, variables, span, LANES),
        ],
        in_specs=[SMEM] + [VMEM] * groups,
        out_specs=[VMEM] * 6 + [HBM],
        scratch_shapes=[
            pltpu.VMEM((count, variables, inside, LANES), f32),
            pltpu.SemaphoreType.DMA((1,)),
        ],
        compiler_params=ROOM,
        cost_estimate=pl.CostEstimate(
            flops=20 * STEPS * span * both * rows, bytes_accessed=2**20, transcendentals=0
        ),
        name="inner",
    )(band_rows, *mine)
    *arrays, inner_result, bands = inner

    def finished(side, halo, bands):
        return pl.pallas_call(
            functools.partial(end_kernel, groups, side),
            out_shape=[
                struct(count, variables, span, LANES),
                struct(halves, both, width, LANES),
            ],
            in_specs=[HBM] + [VMEM] * 6 + [HBM],
            out_specs=[HBM, VMEM],
            input_output_aliases={7: 0},
            scratch_shapes=[pltpu.VMEM((2 * width, both, rows), f32)] * 4
            + [
                pltpu.VMEM((count, variables, width, LANES), f32),
                pltpu.SMEM(band_rows.shape, band_rows.dtype),
                pltpu.SemaphoreType.DMA((groups + 1,)),
            ],
            compiler_params=ROOM,
            name="high_end" if side else "low_end",
        )(band_rows, halo, *arrays, bands)

    bands, low_result = finished(0, low, bands)
    bands, high_result = finished(1, high, bands)
    strips = pl.pallas_call(
        functools.partial(strips_kernel, groups),
        out_shape=[struct(both, width, rows)] * groups,
        in_specs=[VMEM] * 3,
        out_specs=[VMEM] * groups,
        scratch_shapes=[pltpu.VMEM((halves, both, span, LANES), f32)],
        compiler_params=ROOM,
        name="strips",
    )(low_result, inner_result, high_result)
    arrived = lax.all_to_all(bands, "band", split_axis=0, concat_axis=0, tiled=True)
    pieces = exchanged(strips)
    increment, taps, keep = pl.pallas_call(
        functools.partial(increment_kernel, groups),
        out_shape=[
            struct(*background.shape),
            struct(TAPS, variables, levels, 1, count * width),
            jax.ShapeDtypeStruct((CAP, count * width), jnp.int32),
        ],
        in_specs=[SMEM, SMEM] + [VMEM] * groups,
        out_specs=[VMEM] * 3,
        scratch_shapes=[pltpu.VMEM((variables, levels, width, rows), f32)],
        compiler_params=ROOM,
        name="increment",
    )(band_rows, weights, *pieces)
    band_field = pl.pallas_call(
        functools.partial(band_kernel, groups, width),
        out_shape=struct(variables, levels, CAP, count * width),
        in_specs=[VMEM] * 3,
        out_specs=HBM,
        scratch_shapes=[pltpu.VMEM((variables, levels, CAP, count * width), f32)] * 2
        + [pltpu.SemaphoreType.DMA((variables * groups,))],
        compiler_params=ROOM,
        name="bands",
    )(taps, keep, arrived)
    return increment, band_field


def solution(mesh):
    in_specs = (
        P(None, None, ("lon", "band"), None),
        P(None, ("lon", "band"), None),
        P(None, ("lon", "band"), None),
        P(),
        P(),
    )
    out_specs = (P(None, None, ("lon", "band"), None), P(None, None, "band", "lon"))
    return jax.shard_map(
        functools.partial(shards, dict(mesh.shape)),
        mesh=mesh,
        in_specs=in_specs,
        out_specs=out_specs,
        check_vma=False,
    )
```

```python
import functools
import math

import jax
import jax.numpy as jnp
from jax import lax
from jax.experimental import pallas as pl
from jax.experimental.pallas import tpu as pltpu
from jax.sharding import PartitionSpec as P

STEPS = 8
CAP = 32
LANES = 128
TAPS = 5
BLOCK = 16
VMEM = pl.BlockSpec(memory_space=pltpu.VMEM)
SMEM = pl.BlockSpec(memory_space=pltpu.SMEM)
HBM = pl.BlockSpec(memory_space=pltpu.HBM)
ROOM = pltpu.CompilerParams(vmem_limit_bytes=8 * 2**20)


def member(groups):
    return lax.rem(lax.axis_index("band"), groups)


def regroup_kernel(background, scale_x, scale_y, *refs):
    *pieces, sems = refs
    variables, levels = background.shape[:2]
    part = levels // len(pieces)
    me = member(len(pieces))
    copies = []
    for k, piece in enumerate(pieces):
        near = pl.ds(jnp.bitwise_xor(me, k) * part, part)
        sources = [background.at[v, near] for v in range(variables)]
        sources += [scale_x.at[near], scale_y.at[near]]
        for i, source in enumerate(sources):
            target = piece.at[pl.ds(i * part, part)]
            copies.append(pltpu.make_async_copy(source, target, sems.at[k, i]))
    for copy in copies:
        copy.start()
    for copy in copies:
        copy.wait()


def edges_kernel(*refs):
    *pieces, first, last = refs
    groups = len(pieces)
    me = member(groups)
    for k, piece in enumerate(pieces):

        @pl.when(me == k)
        def _(piece=piece):
            first[...] = piece[...]

        @pl.when(me == groups - 1 - k)
        def _(piece=piece):
            last[...] = piece[...]


def spread_out(source, near, field, along_x, along_y, down_y):
    channels, _, rows = source.shape
    part = channels // 4
    pairs = 2 * part
    upper = lax.broadcasted_iota(jnp.int32, (1, pairs, rows), 1) < part
    inside = lax.broadcasted_iota(jnp.int32, (1, pairs, rows), 2) < rows - 1
    flow = jnp.swapaxes(source[...], 0, 1)
    field[near] = flow[:, :pairs]
    coefs = flow[:, pairs:]
    swapped = pltpu.roll(coefs, part, 1)
    along_x[near] = jnp.where(upper, coefs, swapped)
    flow_y = jnp.where(inside, jnp.where(upper, swapped, coefs), 0.0)
    along_y[near] = flow_y
    down_y[near] = pltpu.roll(flow_y, 1, 2)


def advance(parts):
    joined, fluxes, ends = [], [], []
    for field, along_x, along_y, down_y, first, last, before, behind in parts:
        near = pl.ds(first, last - first)
        here = field[near]
        inner = along_x[pl.ds(first, last - first - 1)] * (here[1:] - here[:-1])
        if before is None:
            before = along_x[first - 1] * (here[0] - field[first - 1])
        if behind is None:
            behind = along_x[last - 1] * (field[last] - here[-1])
        fluxes.append((before, behind))
        entering = jnp.concatenate([before[None], inner], 0)
        leaving = jnp.concatenate([inner, behind[None]], 0)
        joined.append((here, leaving, entering, along_y[near], down_y[near]))
        ends.append(sum(ends[-1:]) + last - first)
    here, leaving, entering, up, down = (jnp.concatenate(each, 0) for each in zip(*joined))
    rows = here.shape[-1]
    flux_y = up * (pltpu.roll(here, rows - 1, 2) - here)
    under = down * (here - pltpu.roll(here, 1, 2))
    result = here + leaving - entering + flux_y - under
    for (field, _, _, _, first, last, _, _), end in zip(parts, ends):
        field[pl.ds(first, last - first)] = result[end - last + first : end]
    return fluxes


def turn(columns, result, at):
    block = jnp.swapaxes(columns, 0, 1)
    for half in range(result.shape[0]):
        result[half, :, at] = block[:, :, half * LANES : (half + 1) * LANES]


def pack(result, turned, band_rows, bands, copies):
    halves, channels, count, _ = result.shape
    part = channels // 2
    total = bands.shape[0]
    for half in range(halves):
        for i in range(channels):
            turned[half, i] = pltpu.roll(result[half, i], i % part * CAP, 1)
    lane = lax.broadcasted_iota(jnp.int32, (count, LANES), 1)
    start = jnp.int32(0)
    for b in range(total):
        half = start // LANES
        offset = start - half * LANES
        beyond = lax.rem(half + 1, halves)
        place = jnp.bitwise_and(lane + (LANES - offset), LANES - 1)
        over = jnp.bitwise_and(place, CAP - 1) >= LANES - offset
        for v in range(2):
            here, there = turned[half, v * part], turned[beyond, v * part]
            for l in range(1, part):
                chosen = place >= l * CAP
                here = jnp.where(chosen, turned[half, v * part + l], here)
                there = jnp.where(chosen, turned[beyond, v * part + l], there)
            together = jnp.where(over, there, here)
            bands[b, v] = pltpu.roll(together, lax.rem(LANES - offset, LANES), 1)
        start = start + band_rows[b]
        if (b + 1) * len(copies) % total == 0:
            copies[(b + 1) * len(copies) // total - 1].start()


def inner_kernel(groups, band_rows, *refs):
    pieces, field, along_x, along_y, down_y = refs[:groups], *refs[groups : groups + 4]
    sides, result, bands, ready, turned, sems = refs[groups + 4 :]
    width = pieces[0].shape[1]
    me = member(groups)
    for k, piece in enumerate(pieces):
        near = pl.ds(jnp.bitwise_xor(me, k) * width, width)
        spread_out(piece, near, field, along_x, along_y, down_y)
    span = groups * width
    for step in range(STEPS):
        last = step + 1
        behind = None
        for first in range(step + 1, span - 1 - step, BLOCK):
            last = min(first + BLOCK, span - 1 - step)
            piece = (field, along_x, along_y, down_y, first, last, behind, None)
            before, behind = advance([piece])[0]
            if first == step + 1:
                sides[0, step] = before
        sides[1, step] = behind
    for s in range(1, groups - 1):
        turn(field[pl.ds(s * width, width)], result, pl.ds((s - 1) * width, width))
    copy = pltpu.make_async_copy(ready, bands.at[:, :, pl.ds(0, span - 2 * width)], sems.at[0])
    pack(result, turned, band_rows, ready, [copy])
    copy.wait()


def end_kernel(groups, side, rows_far, halo, *refs):
    inner, sides, _, bands, result = refs[:4], *refs[4:8]
    end, ready, turned, band_rows, sems = refs[8:12], *refs[12:]
    rows_copy = pltpu.make_async_copy(rows_far, band_rows, sems.at[groups])
    rows_copy.start()
    width = halo.shape[1]
    span = groups * width
    spread_out(halo, pl.ds(side * width, width), *end)
    for here, array in zip(end, inner):
        here[pl.ds((1 - side) * width, width)] = array[pl.ds(side * (span - width), width)]
    for step in range(STEPS):
        first = width - 1 - step if side else step + 1
        faces = (sides[1, step], None) if side else (None, sides[0, step])
        advance([(*end, first, first + width, *faces)])
    turn(end[0][pl.ds((1 - side) * width, width)], result, pl.ds(0, width))

    copies = []
    each = bands.shape[0] // groups
    for i in range(groups):
        near = pl.ds(i * each, each)
        target = bands.at[near, :, pl.ds(span - (2 - side) * width, width)]
        copies.append(pltpu.make_async_copy(ready.at[near], target, sems.at[i]))
    rows_copy.wait()
    pack(result, turned, band_rows, ready, copies)
    for copy in copies:
        copy.wait()


def strips_kernel(groups, low, inner, high, *refs):
    strips, whole = refs[:groups], refs[groups]
    halves, _, width, _ = low.shape
    span = groups * width
    me = member(groups)
    whole[:, :, pl.ds(0, width)] = low[...]
    whole[:, :, pl.ds(width, span - 2 * width)] = inner[...]
    whole[:, :, pl.ds(span - width, width)] = high[...]
    for k in range(groups):
        s = jnp.bitwise_xor(me, k)
        for half in range(halves):
            strips[k][:, :, half * LANES : (half + 1) * LANES] = whole[
                half, :, pl.ds(pl.multiple_of(s * width, width), width)
            ]


def filtered(taps, v, l, levels, whole):
    total = whole[v, l]
    for tap in range(TAPS):
        other = l + tap - TAPS // 2
        if 0 <= other < levels:
            total = total + taps(tap, v, l) * whole[v, other]
    return total


def increment_kernel(groups, band_rows, weights, *refs):
    pieces, out, taps, keep, whole = refs[:groups], *refs[groups:]
    variables, levels = out.shape[:2]
    part = levels // groups
    me = member(groups)
    for k in range(groups):
        near = pl.ds(jnp.bitwise_xor(me, k) * part, part)
        for v in range(variables):
            whole[v, near] = pieces[k][pl.ds(v * part, part)]
    for v in range(variables):
        for l in range(levels):
            out[v, l] = filtered(lambda a, b, c: weights[a, b, c], v, l, levels, whole)
            for tap in range(TAPS):
                taps[tap, v, l] = jnp.full(taps.shape[3:], weights[tap, v, l])
    row = lax.broadcasted_iota(jnp.int32, keep.shape, 0)
    keep[...] = (row < band_rows[lax.axis_index("band")]).astype(jnp.int32)


def band_kernel(groups, width, taps, keep, arrived, out, whole, ready, sems):
    variables, levels, height, _ = out.shape
    part = levels // groups
    count, _, span, _ = arrived.shape
    inside = span - 2 * width
    mine = keep[...] > 0
    copies = []
    for v in range(variables):
        for q in range(groups):
            blocks = []
            for s in range(q, count, groups):
                blocks += [arrived[s, v, inside : inside + width], arrived[s, v, :inside]]
                blocks += [arrived[s, v, inside + width :]]
            flat = jnp.transpose(jnp.concatenate(blocks, 0))
            for l in range(part):
                whole[v, q * part + l] = flat[l * height : (l + 1) * height]
    for v in range(variables):
        for l in range(levels):
            total = filtered(lambda a, b, c: taps[a, b, c], v, l, levels, whole)
            ready[v, l] = jnp.where(mine, total, 0.0)
            if (l + 1) % part == 0:
                near = pl.ds(l + 1 - part, part)
                i = len(copies)
                copies.append(
                    pltpu.make_async_copy(ready.at[v, near], out.at[v, near], sems.at[i])
                )
                copies[i].start()
    for copy in copies:
        copy.wait()


def shards(mesh_shape, background, scale_x, scale_y, filter_bands, band_rows):
    variables, levels, width, rows = background.shape
    count, blocks = mesh_shape["band"], mesh_shape["lon"]
    groups = math.isqrt(count)
    part = levels // groups
    channels = (variables + 2) * part
    f32 = jnp.float32

    def struct(*shape):
        return jax.ShapeDtypeStruct(shape, f32)

    piece = struct(channels, width, rows)
    parted = pl.pallas_call(
        regroup_kernel,
        out_shape=[piece] * groups,
        in_specs=[HBM] * 3,
        out_specs=[VMEM] * groups,
        scratch_shapes=[pltpu.SemaphoreType.DMA((groups, variables + 2))],
        compiler_params=ROOM,
        name="regroup",
    )(*(pltpu.with_memory_space_constraint(a, pltpu.HBM) for a in (background, scale_x, scale_y)))
    weights = jnp.transpose(filter_bands, (1, 0, 2))

    def exchanged(pieces):
        return [pieces[0]] + [
            lax.ppermute(pieces[k], "band", [(i, i ^ k) for i in range(count)])
            for k in range(1, groups)
        ]

    mine = exchanged(parted)
    first, last = pl.pallas_call(
        edges_kernel,
        out_shape=[piece] * 2,
        in_specs=[VMEM] * groups,
        out_specs=[VMEM] * 2,
        compiler_params=ROOM,
        name="edges",
    )(*mine)

    def shifted(by):
        total = count * blocks
        pairs = []
        for source in range(total):
            target = (source + by) % total
            pairs.append(
                (
                    source % count * blocks + source // count,
                    target % count * blocks + target // count,
                )
            )
        return pairs

    axes = ("band", "lon")
    low = lax.ppermute(last, axes, shifted(groups))
    high = lax.ppermute(first, axes, shifted(-groups))
    span = groups * width
    inside = span - 2 * width
    halves = rows // LANES
    both = variables * part
    inner = pl.pallas_call(
        functools.partial(inner_kernel, groups),
        out_shape=[struct(span, both, rows)] * 4
        + [
            struct(2, STEPS, both, rows),
            struct(halves, both, inside, LANES),
            struct(count, variables, span, LANES),
        ],
        in_specs=[SMEM] + [VMEM] * groups,
        out_specs=[VMEM] * 6 + [HBM],
        scratch_shapes=[
            pltpu.VMEM((count, variables, inside, LANES), f32),
            pltpu.VMEM((halves, both, inside, LANES), f32),
            pltpu.SemaphoreType.DMA((1,)),
        ],
        compiler_params=ROOM,
        cost_estimate=pl.CostEstimate(
            flops=20 * STEPS * span * both * rows, bytes_accessed=2**20, transcendentals=0
        ),
        name="inner",
    )(band_rows, *mine)
    *arrays, inner_result, bands = inner

    def finished(side, halo, bands):
        return pl.pallas_call(
            functools.partial(end_kernel, groups, side),
            out_shape=[
                struct(count, variables, span, LANES),
                struct(halves, both, width, LANES),
            ],
            in_specs=[HBM] + [VMEM] * 6 + [HBM],
            out_specs=[HBM, VMEM],
            input_output_aliases={7: 0},
            scratch_shapes=[pltpu.VMEM((2 * width, both, rows), f32)] * 4
            + [
                pltpu.VMEM((count, variables, width, LANES), f32),
                pltpu.VMEM((halves, both, width, LANES), f32),
                pltpu.SMEM(band_rows.shape, band_rows.dtype),
                pltpu.SemaphoreType.DMA((groups + 1,)),
            ],
            compiler_params=ROOM,
            name="high_end" if side else "low_end",
        )(band_rows, halo, *arrays, bands)

    bands, low_result = finished(0, low, bands)
    bands, high_result = finished(1, high, bands)
    strips = pl.pallas_call(
        functools.partial(strips_kernel, groups),
        out_shape=[struct(both, width, rows)] * groups,
        in_specs=[VMEM] * 3,
        out_specs=[VMEM] * groups,
        scratch_shapes=[pltpu.VMEM((halves, both, span, LANES), f32)],
        compiler_params=ROOM,
        name="strips",
    )(low_result, inner_result, high_result)
    arrived = lax.all_to_all(bands, "band", split_axis=0, concat_axis=0, tiled=True)
    pieces = exchanged(strips)
    increment, taps, keep = pl.pallas_call(
        functools.partial(increment_kernel, groups),
        out_shape=[
            struct(*background.shape),
            struct(TAPS, variables, levels, 1, count * width),
            jax.ShapeDtypeStruct((CAP, count * width), jnp.int32),
        ],
        in_specs=[SMEM, SMEM] + [VMEM] * groups,
        out_specs=[VMEM] * 3,
        scratch_shapes=[pltpu.VMEM((variables, levels, width, rows), f32)],
        compiler_params=ROOM,
        name="increment",
    )(band_rows, weights, *pieces)
    band_field = pl.pallas_call(
        functools.partial(band_kernel, groups, width),
        out_shape=struct(variables, levels, CAP, count * width),
        in_specs=[VMEM] * 3,
        out_specs=HBM,
        scratch_shapes=[pltpu.VMEM((variables, levels, CAP, count * width), f32)] * 2
        + [pltpu.SemaphoreType.DMA((variables * groups,))],
        compiler_params=ROOM,
        name="bands",
    )(taps, keep, arrived)
    return increment, band_field


def solution(mesh):
    in_specs = (
        P(None, None, ("lon", "band"), None),
        P(None, ("lon", "band"), None),
        P(None, ("lon", "band"), None),
        P(),
        P(),
    )
    out_specs = (P(None, None, ("lon", "band"), None), P(None, None, "band", "lon"))
    return jax.shard_map(
        functools.partial(shards, dict(mesh.shape)),
        mesh=mesh,
        in_specs=in_specs,
        out_specs=out_specs,
        check_vma=False,
    )
```

```python
import functools
import math

import jax
import jax.numpy as jnp
from jax import lax
from jax.experimental import pallas as pl
from jax.experimental.pallas import tpu as pltpu
from jax.sharding import PartitionSpec as P

STEPS = 8
CAP = 32
LANES = 128
TAPS = 5
BLOCK = 16
VMEM = pl.BlockSpec(memory_space=pltpu.VMEM)
SMEM = pl.BlockSpec(memory_space=pltpu.SMEM)
HBM = pl.BlockSpec(memory_space=pltpu.HBM)
ROOM = pltpu.CompilerParams(vmem_limit_bytes=8 * 2**20)


def member(groups):
    return lax.rem(lax.axis_index("band"), groups)


def partners(groups, odd):
    between = list(range(1, groups - 1))
    return [0, groups - 1] + (between[::-1] if odd else between)


def partner(groups, i):
    odd = lax.rem(lax.axis_index("lon"), 2) == 1
    return jnp.where(odd, partners(groups, True)[i], partners(groups, False)[i])


def regroup_kernel(background, scale_x, scale_y, *refs):
    *pieces, field, along_x, along_y, sems = refs
    variables, levels = background.shape[:2]
    part = levels // len(pieces)
    me = member(len(pieces))
    parts, copies = [], []
    for k in range(len(pieces)):
        near = pl.ds(jnp.bitwise_xor(me, partner(len(pieces), k)) * part, part)
        parts.append(near)
        copies.append(
            [
                pltpu.make_async_copy(background.at[:, near], field.at[:, near], sems.at[k, 0]),
                pltpu.make_async_copy(scale_x.at[near], along_x.at[near], sems.at[k, 1]),
                pltpu.make_async_copy(scale_y.at[near], along_y.at[near], sems.at[k, 2]),
            ]
        )
        for copy in copies[k]:
            copy.start()
    for near, piece, each in zip(parts, pieces, copies):
        for copy in each:
            copy.wait()
        sources = [field[v, near] for v in range(variables)]
        sources += [along_x[near], along_y[near]]
        piece[...] = jnp.swapaxes(jnp.concatenate(sources, 0), 0, 1)


def edges_kernel(*refs):
    *pieces, first, last = refs
    groups = len(pieces)
    me = member(groups)
    for i, piece in enumerate(pieces):
        apart = jnp.bitwise_xor(me, partner(groups, i))

        @pl.when(apart == 0)
        def _(piece=piece):
            first[...] = piece[...]

        @pl.when(apart == groups - 1)
        def _(piece=piece):
            last[...] = piece[...]


def spread_out(source, near, field, along_x, along_y, down_y):
    _, channels, rows = source.shape
    part = channels // 4
    pairs = 2 * part
    upper = lax.broadcasted_iota(jnp.int32, (1, pairs, rows), 1) < part
    inside = lax.broadcasted_iota(jnp.int32, (1, pairs, rows), 2) < rows - 1
    field[near] = source[:, :pairs]
    coefs = source[:, pairs:]
    swapped = pltpu.roll(coefs, part, 1)
    along_x[near] = jnp.where(upper, coefs, swapped)
    flow_y = jnp.where(inside, jnp.where(upper, swapped, coefs), 0.0)
    along_y[near] = flow_y
    down_y[near] = pltpu.roll(flow_y, 1, 2)


def advance(parts):
    joined, fluxes, ends = [], [], []
    for field, along_x, along_y, down_y, first, last, before, behind in parts:
        near = pl.ds(first, last - first)
        here = field[near]
        inner = along_x[pl.ds(first, last - first - 1)] * (here[1:] - here[:-1])
        if before is None:
            before = along_x[first - 1] * (here[0] - field[first - 1])
        if behind is None:
            behind = along_x[last - 1] * (field[last] - here[-1])
        fluxes.append((before, behind))
        entering = jnp.concatenate([before[None], inner], 0)
        leaving = jnp.concatenate([inner, behind[None]], 0)
        joined.append((here, leaving, entering, along_y[near], down_y[near]))
        ends.append(sum(ends[-1:]) + last - first)
    here, leaving, entering, up, down = (jnp.concatenate(each, 0) for each in zip(*joined))
    rows = here.shape[-1]
    flux_y = up * (pltpu.roll(here, rows - 1, 2) - here)
    under = down * (here - pltpu.roll(here, 1, 2))
    result = here + leaving - entering + flux_y - under
    for (field, _, _, _, first, last, _, _), end in zip(parts, ends):
        field[pl.ds(first, last - first)] = result[end - last + first : end]
    return fluxes


def turn(columns, result, at):
    block = jnp.swapaxes(columns, 0, 1)
    for half in range(result.shape[0]):
        result[half, :, at] = block[:, :, half * LANES : (half + 1) * LANES]


def pack(result, band_rows, bands, copies):
    halves, channels, count, _ = result.shape
    part = channels // 2
    total = bands.shape[0]
    lane = lax.broadcasted_iota(jnp.int32, (count, LANES), 1)
    start = jnp.int32(0)
    for b in range(total):
        half = start // LANES
        offset = start - half * LANES
        beyond = lax.rem(half + 1, halves)
        for v in range(2):
            packed = None
            for l in range(part):
                i = v * part + l
                window = jnp.where(lane >= offset, result[half, i], result[beyond, i])
                shift = lax.rem(LANES + l * CAP - offset, LANES)
                turned = pltpu.roll(window, shift, 1)
                packed = turned if l == 0 else jnp.where(lane >= l * CAP, turned, packed)
            bands[b, v] = packed
        start = start + band_rows[b]
        if (b + 1) * len(copies) % total == 0:
            copies[(b + 1) * len(copies) // total - 1].start()


def inner_kernel(groups, band_rows, *refs):
    pieces, field, along_x, along_y, down_y = refs[:groups], *refs[groups : groups + 4]
    sides, result, bands, ready, sems = refs[groups + 4 :]
    width = pieces[0].shape[0]
    me = member(groups)
    for k, piece in enumerate(pieces):
        near = pl.ds(jnp.bitwise_xor(me, partner(groups, k)) * width, width)
        spread_out(piece, near, field, along_x, along_y, down_y)
    span = groups * width
    for step in range(STEPS):
        last = step + 1
        behind = None
        for first in range(step + 1, span - 1 - step, BLOCK):
            last = min(first + BLOCK, span - 1 - step)
            piece = (field, along_x, along_y, down_y, first, last, behind, None)
            before, behind = advance([piece])[0]
            if first == step + 1:
                sides[0, step] = before
        sides[1, step] = behind
    for s in range(1, groups - 1):
        turn(field[pl.ds(s * width, width)], result, pl.ds((s - 1) * width, width))
    copy = pltpu.make_async_copy(ready, bands.at[:, :, pl.ds(0, span - 2 * width)], sems.at[0])
    pack(result, band_rows, ready, [copy])
    copy.wait()


def end_kernel(groups, side, rows_far, halo, *refs):
    inner, sides, _, bands, result = refs[:4], *refs[4:8]
    end, ready, band_rows, sems = refs[8:12], *refs[12:]
    rows_copy = pltpu.make_async_copy(rows_far, band_rows, sems.at[groups])
    rows_copy.start()
    width = halo.shape[0]
    span = groups * width
    spread_out(halo, pl.ds(side * width, width), *end)
    for here, array in zip(end, inner):
        here[pl.ds((1 - side) * width, width)] = array[pl.ds(side * (span - width), width)]
    for step in range(STEPS):
        first = width - 1 - step if side else step + 1
        faces = (sides[1, step], None) if side else (None, sides[0, step])
        advance([(*end, first, first + width, *faces)])
    turn(end[0][pl.ds((1 - side) * width, width)], result, pl.ds(0, width))

    copies = []
    each = bands.shape[0] // groups
    for i in range(groups):
        near = pl.ds(i * each, each)
        target = bands.at[near, :, pl.ds(span - (2 - side) * width, width)]
        copies.append(pltpu.make_async_copy(ready.at[near], target, sems.at[i]))
    rows_copy.wait()
    pack(result, band_rows, ready, copies)
    for copy in copies:
        copy.wait()


def strips_kernel(groups, low, inner, high, *refs):
    strips, whole = refs[:groups], refs[groups]
    halves, _, width, _ = low.shape
    span = groups * width
    me = member(groups)
    whole[:, :, pl.ds(0, width)] = low[...]
    whole[:, :, pl.ds(width, span - 2 * width)] = inner[...]
    whole[:, :, pl.ds(span - width, width)] = high[...]
    for k in range(groups):
        s = jnp.bitwise_xor(me, k)
        for half in range(halves):
            strips[k][:, :, half * LANES : (half + 1) * LANES] = whole[
                half, :, pl.ds(pl.multiple_of(s * width, width), width)
            ]


def filtered(taps, v, l, levels, whole):
    total = whole[v, l]
    for tap in range(TAPS):
        other = l + tap - TAPS // 2
        if 0 <= other < levels:
            total = total + taps(tap, v, l) * whole[v, other]
    return total


def increment_kernel(groups, band_rows, weights, *refs):
    pieces, out, taps, keep, whole = refs[:groups], *refs[groups:]
    variables, levels = out.shape[:2]
    part = levels // groups
    me = member(groups)
    for k in range(groups):
        near = pl.ds(jnp.bitwise_xor(me, k) * part, part)
        for v in range(variables):
            whole[v, near] = pieces[k][pl.ds(v * part, part)]
    for v in range(variables):
        for l in range(levels):
            out[v, l] = filtered(lambda a, b, c: weights[a, b, c], v, l, levels, whole)
            for tap in range(TAPS):
                taps[tap, v, l] = jnp.full(taps.shape[3:], weights[tap, v, l])
    row = lax.broadcasted_iota(jnp.int32, keep.shape, 0)
    keep[...] = (row < band_rows[lax.axis_index("band")]).astype(jnp.int32)


def band_kernel(groups, width, taps, keep, arrived, out, whole, ready, sems):
    variables, levels, height, _ = out.shape
    part = levels // groups
    count, _, span, _ = arrived.shape
    inside = span - 2 * width
    mine = keep[...] > 0
    copies = []
    for v in range(variables):
        for q in range(groups):
            blocks = []
            for s in range(q, count, groups):
                blocks += [arrived[s, v, inside : inside + width], arrived[s, v, :inside]]
                blocks += [arrived[s, v, inside + width :]]
            flat = jnp.transpose(jnp.concatenate(blocks, 0))
            for l in range(part):
                whole[v, q * part + l] = flat[l * height : (l + 1) * height]
    for v in range(variables):
        for l in range(levels):
            total = filtered(lambda a, b, c: taps[a, b, c], v, l, levels, whole)
            ready[v, l] = jnp.where(mine, total, 0.0)
            if (l + 1) % part == 0:
                near = pl.ds(l + 1 - part, part)
                i = len(copies)
                copies.append(
                    pltpu.make_async_copy(ready.at[v, near], out.at[v, near], sems.at[i])
                )
                copies[i].start()
    for copy in copies:
        copy.wait()


def shards(mesh_shape, background, scale_x, scale_y, filter_bands, band_rows):
    variables, levels, width, rows = background.shape
    count, blocks = mesh_shape["band"], mesh_shape["lon"]
    groups = math.isqrt(count)
    part = levels // groups
    channels = (variables + 2) * part
    f32 = jnp.float32

    def struct(*shape):
        return jax.ShapeDtypeStruct(shape, f32)

    piece = struct(width, channels, rows)
    parted = pl.pallas_call(
        regroup_kernel,
        out_shape=[piece] * groups,
        in_specs=[HBM] * 3,
        out_specs=[VMEM] * groups,
        scratch_shapes=[pltpu.VMEM(a.shape, f32) for a in (background, scale_x, scale_y)]
        + [pltpu.SemaphoreType.DMA((groups, 3))],
        compiler_params=ROOM,
        name="regroup",
    )(*(pltpu.with_memory_space_constraint(a, pltpu.HBM) for a in (background, scale_x, scale_y)))
    weights = jnp.transpose(filter_bands, (1, 0, 2))

    def exchanged(pieces):
        return [pieces[0]] + [
            lax.ppermute(pieces[k], "band", [(i, i ^ k) for i in range(count)])
            for k in range(1, groups)
        ]

    crossed = [partners(groups, lon % 2 == 1) for lon in range(blocks)]
    mine = [parted[0]] + [
        lax.ppermute(
            parted[i],
            ("band", "lon"),
            [
                (band * blocks + lon, (band ^ crossed[lon][i]) * blocks + lon)
                for band in range(count)
                for lon in range(blocks)
            ],
        )
        for i in range(1, groups)
    ]
    first, last = pl.pallas_call(
        edges_kernel,
        out_shape=[piece] * 2,
        in_specs=[VMEM] * groups,
        out_specs=[VMEM] * 2,
        compiler_params=ROOM,
        name="edges",
    )(*mine)

    def shifted(by):
        total = count * blocks
        pairs = []
        for source in range(total):
            target = (source + by) % total
            pairs.append(
                (
                    source % count * blocks + source // count,
                    target % count * blocks + target // count,
                )
            )
        return pairs

    axes = ("band", "lon")
    low = lax.ppermute(last, axes, shifted(groups))
    high = lax.ppermute(first, axes, shifted(-groups))
    span = groups * width
    inside = span - 2 * width
    halves = rows // LANES
    both = variables * part
    inner = pl.pallas_call(
        functools.partial(inner_kernel, groups),
        out_shape=[struct(span, both, rows)] * 4
        + [
            struct(2, STEPS, both, rows),
            struct(halves, both, inside, LANES),
            struct(count, variables, span, LANES),
        ],
        in_specs=[SMEM] + [VMEM] * groups,
        out_specs=[VMEM] * 6 + [HBM],
        scratch_shapes=[
            pltpu.VMEM((count, variables, inside, LANES), f32),
            pltpu.SemaphoreType.DMA((1,)),
        ],
        compiler_params=ROOM,
        cost_estimate=pl.CostEstimate(
            flops=20 * STEPS * span * both * rows, bytes_accessed=2**20, transcendentals=0
        ),
        name="inner",
    )(band_rows, *mine)
    *arrays, inner_result, bands = inner

    def finished(side, halo, bands):
        return pl.pallas_call(
            functools.partial(end_kernel, groups, side),
            out_shape=[
                struct(count, variables, span, LANES),
                struct(halves, both, width, LANES),
            ],
            in_specs=[HBM] + [VMEM] * 6 + [HBM],
            out_specs=[HBM, VMEM],
            input_output_aliases={7: 0},
            scratch_shapes=[pltpu.VMEM((2 * width, both, rows), f32)] * 4
            + [
                pltpu.VMEM((count, variables, width, LANES), f32),
                pltpu.SMEM(band_rows.shape, band_rows.dtype),
                pltpu.SemaphoreType.DMA((groups + 1,)),
            ],
            compiler_params=ROOM,
            name="high_end" if side else "low_end",
        )(band_rows, halo, *arrays, bands)

    bands, low_result = finished(0, low, bands)
    bands, high_result = finished(1, high, bands)
    strips = pl.pallas_call(
        functools.partial(strips_kernel, groups),
        out_shape=[struct(both, width, rows)] * groups,
        in_specs=[VMEM] * 3,
        out_specs=[VMEM] * groups,
        scratch_shapes=[pltpu.VMEM((halves, both, span, LANES), f32)],
        compiler_params=ROOM,
        name="strips",
    )(low_result, inner_result, high_result)
    arrived = lax.all_to_all(bands, "band", split_axis=0, concat_axis=0, tiled=True)
    pieces = exchanged(strips)
    increment, taps, keep = pl.pallas_call(
        functools.partial(increment_kernel, groups),
        out_shape=[
            struct(*background.shape),
            struct(TAPS, variables, levels, 1, count * width),
            jax.ShapeDtypeStruct((CAP, count * width), jnp.int32),
        ],
        in_specs=[SMEM, SMEM] + [VMEM] * groups,
        out_specs=[VMEM] * 3,
        scratch_shapes=[pltpu.VMEM((variables, levels, width, rows), f32)],
        compiler_params=ROOM,
        name="increment",
    )(band_rows, weights, *pieces)
    band_field = pl.pallas_call(
        functools.partial(band_kernel, groups, width),
        out_shape=struct(variables, levels, CAP, count * width),
        in_specs=[VMEM] * 3,
        out_specs=HBM,
        scratch_shapes=[pltpu.VMEM((variables, levels, CAP, count * width), f32)] * 2
        + [pltpu.SemaphoreType.DMA((variables * groups,))],
        compiler_params=ROOM,
        name="bands",
    )(taps, keep, arrived)
    return increment, band_field


def solution(mesh):
    in_specs = (
        P(None, None, ("lon", "band"), None),
        P(None, ("lon", "band"), None),
        P(None, ("lon", "band"), None),
        P(),
        P(),
    )
    out_specs = (P(None, None, ("lon", "band"), None), P(None, None, "band", "lon"))
    return jax.shard_map(
        functools.partial(shards, dict(mesh.shape)),
        mesh=mesh,
        in_specs=in_specs,
        out_specs=out_specs,
        check_vma=False,
    )
```
